128 devices in a mesh: ep: 8 (over z, core), dp: 16 (over y, x).
Axes of the slice: x: 4, y: 4, z: 4, core: 2. Of those that a mesh axis runs over, the one named last changes fastest.
Arguments:
- tokens: bfloat16 [32768, 7168], P(('ep', 'dp')), may hold values from -6 to 6
- grad_out: bfloat16 [32768, 7168], P(('ep', 'dp')), may hold values from -6 to 6
- route_ids: int32 [32768, 8], P(('ep', 'dp')), may hold values from 0 to 255, as said below
- route_probs: float32 [32768, 8], P(('ep', 'dp')), may hold values from 0.1 to 1
- replica_pick: int32 [32768, 8], P(('ep', 'dp')), may hold values from 0 to 1, as said below
- plan: int32 [8], replicated, may hold values from 0 to 5, as said below
- w_gate: bfloat16 [8, 7168, 2048], P('ep', 'dp'), may hold values from -0.0625 to 0.0625
- w_up: bfloat16 [8, 7168, 2048], P('ep', 'dp'), may hold values from -0.0625 to 0.0625
- w_down: bfloat16 [8, 2048, 7168], P('ep', None, 'dp'), may hold values from -0.125 to 0.125
Outputs:
- grad_tokens: bfloat16 [32768, 7168], P(('ep', 'dp'))
- grad_gate: bfloat16 [8, 7168, 2048], P('ep', 'dp')
- grad_up: bfloat16 [8, 7168, 2048], P('ep', 'dp')
- grad_down: bfloat16 [8, 2048, 7168], P('ep', None, 'dp')
The draws below stay inside these ranges and needn't reach their ends.
Inputs may be any that keep to these rules, and one draw needn't show every extreme that they name: `route_ids`: each row names 8 different experts; ids under 6 are the experts held here, and each of them appears in some row of every block of 256 tokens. `replica_pick`: under this pick no replica receives more than 6 of one device's rows, and in every device's rows some replica receives exactly 6. `plan`: every expert under 6 is held by one or two slots; exactly 2 experts are held by two.
All inputs are finite; a program needn't handle non-finite values.
Results may differ from the reference program's by a relative error of at most 0.029.
Values may be sent and summed in bfloat16 or wider, within the bound.
No kernel may reach another device: no remote copies, remote signals or barrier semaphores. Data moves between devices by JAX's collectives and lax.ppermute only.
A program may use at most 128 MiB of HBM per device.

```python
import math
import jax
import jax.numpy as jnp
from jax import lax

D = 7168
F = 2048
ALL = 256
TOP = 8
HOT = 2
MOST = 6
TOK_DEV = 256
REPLICAS = 8
EXPERTS = 6
TOKENS = 32768
DB = 448
ROWS = 768
N_EP = 8
N_DP = 16


def plan_parts(key):
    hot_experts = jax.random.permutation(jax.random.fold_in(key, 11), EXPERTS)[:HOT].astype(jnp.int32)
    slot_experts = jnp.concatenate([jnp.arange(EXPERTS, dtype=jnp.int32), hot_experts])
    shuffle = jax.random.permutation(jax.random.fold_in(key, 12), REPLICAS)
    return (slot_experts[shuffle].astype(jnp.int32), hot_experts)


def route_parts(key):
    placement, hot_experts = plan_parts(key)
    blocks = TOKENS // TOK_DEV
    expert_ids = jnp.arange(EXPERTS, dtype=jnp.int32)
    is_hot = jnp.any(expert_ids[:, None] == hot_experts[None, :], axis=1)
    ceiling = jnp.where(is_hot, 2 * MOST, MOST).astype(jnp.int32)
    counts = jax.random.randint(jax.random.fold_in(key, 21), (blocks, EXPERTS), 1, ceiling[None, :] + 1).astype(jnp.int32)
    filled = jax.random.randint(jax.random.fold_in(key, 22), (blocks,), 0, EXPERTS).astype(jnp.int32)
    counts = jnp.where(expert_ids[None, :] == filled[:, None], ceiling[None, :], counts)
    scores = jax.random.randint(jax.random.fold_in(key, 23), (blocks, EXPERTS, TOK_DEV), 0, 2 ** 15).astype(jnp.int32)
    scores = scores * TOK_DEV + jnp.arange(TOK_DEV, dtype=jnp.int32)
    ranks = jnp.argsort(jnp.argsort(scores, axis=-1), axis=-1).astype(jnp.int32)
    present = ranks < counts[..., None]
    second = (ranks >= (counts[..., None] + 1) // 2).astype(jnp.int32)
    present_rows = present.transpose(0, 2, 1).reshape(TOKENS, EXPERTS)
    second_rows = second.transpose(0, 2, 1).reshape(TOKENS, EXPERTS)
    noise_rank = jax.random.randint(jax.random.fold_in(key, 24), (TOKENS, ALL), 0, 2 ** 15).astype(jnp.int32)
    noise_rank = noise_rank * ALL + jnp.arange(ALL, dtype=jnp.int32)
    window = jnp.where(present_rows, 2 ** 28 + expert_ids[None, :], -1 - expert_ids[None, :])
    priority = jnp.concatenate([window, noise_rank[:, EXPERTS:]], axis=1)
    chosen_ids = lax.top_k(priority, TOP)[1].astype(jnp.int32)
    clipped = jnp.minimum(chosen_ids, EXPERTS - 1)
    spare_pick = jax.random.randint(jax.random.fold_in(key, 25), (TOKENS, TOP), 0, 2).astype(jnp.int32)
    picked = jnp.where(chosen_ids < EXPERTS, jnp.take_along_axis(second_rows, clipped, axis=1), spare_pick)
    return (chosen_ids, picked.astype(jnp.int32))


def draw_plan(key, part):
    return plan_parts(key)[0]


def draw_route_ids(key, part):
    return route_parts(key)[0]


def draw_replica_pick(key, part):
    return route_parts(key)[1]


def block_levels(own_key, extent, shards, least, largest):
    factor_of = 1.0
    for dim, blocks in shards:
        steps = jax.random.uniform(jax.random.fold_in(jax.random.fold_in(own_key, 6), dim), (blocks,), jnp.float32, least / len(shards), largest / len(shards))
        factor_of = factor_of * jnp.repeat(jnp.exp(steps), extent[dim] // blocks).reshape((-1,) + (1,) * (len(extent) - 1 - dim))
    return factor_of


def centred(key, extent, scale, bound, split=(), kind=jnp.bfloat16):
    drawn = scale * jax.random.normal(key, extent, jnp.float32)
    if split:
        drawn = drawn * block_levels(key, extent, split, -0.22, 0.18)
    return jnp.clip(drawn, -bound, bound).astype(kind)


def setup_inputs(seed: int = 0) -> dict:
    seeds = jax.random.split(jax.random.key(seed), 10)
    return {
        "tokens": centred(seeds[0], (TOKENS, D), 1.0, 6.0, ((0, 128),)),
        "grad_out": centred(seeds[1], (TOKENS, D), 1.0, 6.0, ((0, 128),)),
        "route_ids": draw_route_ids(jax.random.fold_in(seeds[9], 71), 0),
        "route_probs": jnp.clip(jnp.exp(math.log(1.0) - 2.3025851 * jax.random.uniform(seeds[3], (TOKENS, TOP), jnp.float32) ** block_levels(seeds[3], (TOKENS, TOP), ((0, 128),), -0.2, 0.2)), 0.1, 1.0),
        "replica_pick": draw_replica_pick(jax.random.fold_in(seeds[9], 71), 0),
        "plan": draw_plan(jax.random.fold_in(seeds[9], 71), 0),
        "w_gate": centred(seeds[6], (REPLICAS, D, F), D ** -0.5, 0.0625, ((0, 8), (1, 16))),
        "w_up": centred(seeds[7], (REPLICAS, D, F), D ** -0.5, 0.0625, ((0, 8), (1, 16))),
        "w_down": centred(seeds[8], (REPLICAS, F, D), F ** -0.5, 0.125, ((0, 8), (2, 16))),
    }


def routing_targets(route_ids, replica_pick, placement, expert_count):
    replicas = placement.shape[0]
    expert_ids = jnp.arange(expert_count, dtype=jnp.int32)
    owner_table = (placement[None, :] == expert_ids[:, None]).astype(jnp.int32)
    copies = jnp.sum(owner_table, axis=1)
    before = jnp.cumsum(owner_table, axis=1) - owner_table
    replica_rank = jnp.sum(owner_table * before, axis=0)
    inside = route_ids < expert_count
    clipped = jnp.minimum(route_ids, expert_count - 1)
    chosen = clipped[..., None] == expert_ids
    copies_row = jnp.sum(jnp.where(chosen, copies, 0), axis=-1)
    wanted = replica_pick % copies_row
    matched = (placement == clipped[..., None]) & (replica_rank == wanted[..., None]) & inside[..., None]
    replica_ids = jnp.arange(replicas, dtype=jnp.int32)
    found = jnp.any(matched, axis=-1).astype(jnp.int32)
    return jnp.sum(jnp.where(matched, replica_ids, 0), axis=-1) + replicas * (1 - found)


def slot_codes(flat_target, replicas, capacity):
    replica_ids = jnp.arange(replicas, dtype=jnp.int32)
    onehot = (flat_target[:, None] == replica_ids[None, :]).astype(jnp.int32)
    before = jnp.cumsum(onehot, axis=0) - onehot
    slot_rank = jnp.sum(before * onehot, axis=1)
    return jnp.where(flat_target < replicas, flat_target * capacity + slot_rank, replicas * capacity)


def selectors(row_codes, weights_in, count):
    slot_ids = jnp.arange(count, dtype=jnp.int32)
    matched = row_codes[None, :, :] == slot_ids[:, None, None]
    select = jnp.any(matched, axis=-1).astype(jnp.bfloat16)
    row_scale = jnp.sum(jnp.where(matched, weights_in[None, :, :], jnp.float32(0.0)), axis=(1, 2))
    return select, row_scale


def rounded(value):
    return lax.optimization_barrier(value.astype(jnp.bfloat16)).astype(jnp.float32)


def backward_units(gate, up_val, hidden_grad):
    sigmoid_gate = jax.nn.sigmoid(gate)
    activated = gate * sigmoid_gate
    hidden = (activated * up_val).astype(jnp.bfloat16)
    up_grad = (hidden_grad * activated).astype(jnp.bfloat16)
    gate_grad = (hidden_grad * up_val * sigmoid_gate * (1.0 + gate * (1.0 - sigmoid_gate))).astype(jnp.bfloat16)
    return hidden, gate_grad, up_grad


def expert_backward(inputs):
    rows_in, rows_grad, gate_w, up_w, down_w = inputs
    count = rows_in.shape[0]
    left_in = rows_in.reshape(count, N_DP, DB).astype(jnp.float32)
    left_grad = rows_grad.reshape(count, N_DP, DB).astype(jnp.float32)
    gate_parts = jnp.einsum("rbd,bdf->brf", left_in, gate_w.reshape(N_DP, DB, F).astype(jnp.float32))
    gate = jnp.sum(rounded(gate_parts), axis=0)
    up_parts = jnp.einsum("rbd,bdf->brf", left_in, up_w.reshape(N_DP, DB, F).astype(jnp.float32))
    up_val = jnp.sum(rounded(up_parts), axis=0)
    down_parts = jnp.einsum("rbd,fbd->brf", left_grad, down_w.reshape(F, N_DP, DB).astype(jnp.float32))
    hidden_grad = jnp.sum(rounded(down_parts), axis=0)
    hidden, gate_grad, up_grad = backward_units(gate, up_val, hidden_grad)
    contract_rows = (((0,), (0,)), ((), ()))
    term_down = lax.dot_general(hidden, rows_grad, contract_rows, preferred_element_type=jnp.float32)
    term_gate = lax.dot_general(rows_in, gate_grad, contract_rows, preferred_element_type=jnp.float32)
    term_up = lax.dot_general(rows_in, up_grad, contract_rows, preferred_element_type=jnp.float32)
    contract_units = (((1,), (1,)), ((), ()))
    row_grads = lax.dot_general(gate_grad, gate_w, contract_units, preferred_element_type=jnp.float32)
    row_grads = row_grads + lax.dot_general(up_grad, up_w, contract_units, preferred_element_type=jnp.float32)
    return (row_grads.astype(jnp.bfloat16), term_gate.astype(jnp.bfloat16),
            term_up.astype(jnp.bfloat16), term_down.astype(jnp.bfloat16))


def replica_total(same_table, replica_terms):
    def one_row(weights_row):
        return jnp.tensordot(weights_row, replica_terms.astype(jnp.float32), axes=1).astype(jnp.bfloat16)
    return lax.map(one_row, same_table)


def reference(tokens, grad_out, route_ids, route_probs, replica_pick, plan, w_gate, w_up, w_down):
    replicas = plan.shape[0]
    blocks = N_EP * N_DP
    slot_total = replicas * MOST
    target = routing_targets(route_ids, replica_pick, plan, EXPERTS)
    flat_codes = jax.vmap(lambda rows: slot_codes(rows, replicas, MOST))(target.reshape(blocks, TOK_DEV * TOP))
    block_codes = flat_codes.reshape(blocks, TOK_DEV, TOP)
    block_probs = route_probs.reshape(blocks, TOK_DEV, TOP)
    select, row_scale = jax.vmap(lambda codes_in, probs_in: selectors(codes_in, probs_in, slot_total))(block_codes, block_probs)
    token_blocks = tokens.reshape(blocks, TOK_DEV, D)
    grad_blocks = grad_out.reshape(blocks, TOK_DEV, D)

    def gather_block(inputs):
        chooser, scaling, token_rows, grad_rows = inputs
        rows_in = jnp.dot(chooser, token_rows, preferred_element_type=jnp.float32).astype(jnp.bfloat16)
        rows_grad = (jnp.dot(chooser, grad_rows, preferred_element_type=jnp.float32) * scaling[:, None]).astype(jnp.bfloat16)
        return rows_in, rows_grad

    buffer_in, buffer_grad = lax.map(gather_block, (select, row_scale, token_blocks, grad_blocks))
    buffer_in = buffer_in.reshape(blocks, replicas, MOST, D).transpose(1, 0, 2, 3).reshape(replicas, ROWS, D)
    buffer_grad = buffer_grad.reshape(blocks, replicas, MOST, D).transpose(1, 0, 2, 3).reshape(replicas, ROWS, D)
    row_grads, term_gate, term_up, term_down = lax.map(expert_backward, (buffer_in, buffer_grad, w_gate, w_up, w_down))
    same_table = (plan[:, None] == plan[None, :]).astype(jnp.float32)
    grad_gate = replica_total(same_table, term_gate)
    grad_up = replica_total(same_table, term_up)
    grad_down = replica_total(same_table, term_down)
    returned = row_grads.reshape(replicas, blocks, MOST, D).transpose(1, 0, 2, 3).reshape(blocks, slot_total, D)

    def combine_block(inputs):
        chooser, rows_back = inputs
        summed = lax.dot_general(chooser, rows_back, (((0,), (0,)), ((), ())), preferred_element_type=jnp.float32)
        return summed.astype(jnp.bfloat16)

    grad_tokens = lax.map(combine_block, (select, returned)).reshape(TOKENS, D)
    return grad_tokens, grad_gate, grad_up, grad_down
```

```python
import functools
import itertools

import jax
import jax.numpy as jnp
import numpy as np
from jax import lax
from jax.experimental import pallas as pl
from jax.experimental.pallas import tpu as pltpu
from jax.sharding import PartitionSpec as P

MOST = 6
PAD = 8
CHUNKS = (1024, 1024)
CONTRACT_ROWS = (((0,), (0,)), ((), ()))
CONTRACT_UNITS = (((1,), (1,)), ((), ()))


def pairings(replicas):
    tables = []
    pairs = list(itertools.combinations(range(replicas), 2))
    for first, second in itertools.combinations(pairs, 2):
        if not set(first) & set(second):
            partner = list(range(replicas))
            for a, b in (first, second):
                partner[a], partner[b] = b, a
            tables.append(partner)
    return tables


def dispatch_kernel(ids_ref, pick_ref, probs_ref, plan_ref, tok_ref, grad_ref, send_ref, sel_ref, scale_ref):
    replicas = plan_ref.shape[0]
    tokens = ids_ref.shape[1]

    @pl.when(pl.program_id(0) == 0)
    def _():
        ids = ids_ref[...]
        pick = pick_ref[...]
        probs = probs_ref[...]
        hits, weights = [], []
        for r in range(replicas):
            expert = plan_ref[r]
            copies = jnp.int32(0)
            rank = jnp.int32(0)
            for other in range(replicas):
                same = (plan_ref[other] == expert).astype(jnp.int32)
                copies += same
                if other < r:
                    rank += same
            wanted = jnp.where(copies > 1, lax.rem(pick, jnp.int32(2)), 0)
            matched = (ids == expert) & (wanted == rank)
            hits.append(jnp.max(jnp.where(matched, 1.0, 0.0), axis=0, keepdims=True))
            weights.append(jnp.sum(jnp.where(matched, probs, 0.0), axis=0, keepdims=True))
        hit = jnp.concatenate(hits, axis=0)
        earlier = lax.broadcasted_iota(jnp.int32, (tokens, tokens), 0) < lax.broadcasted_iota(
            jnp.int32, (tokens, tokens), 1
        )
        before = jnp.dot(
            hit.astype(jnp.bfloat16),
            earlier.astype(jnp.float32).astype(jnp.bfloat16),
            preferred_element_type=jnp.float32,
        )
        slot = lax.broadcasted_iota(jnp.int32, (PAD, tokens), 0).astype(jnp.float32)
        rows, scales = [], []
        for r in range(replicas):
            chosen = jnp.where((before[r : r + 1] == slot) & (hit[r : r + 1] > 0.0), 1.0, 0.0)
            rows.append(chosen)
            scales.append(jnp.sum(chosen * weights[r], axis=1, keepdims=True))
        sel_ref[...] = jnp.concatenate(rows, axis=0).astype(jnp.bfloat16)
        scale_ref[...] = jnp.broadcast_to(jnp.concatenate(scales, axis=0), scale_ref.shape)

    sel = sel_ref[...]
    rows_in = jnp.dot(sel, tok_ref[...], preferred_element_type=jnp.float32)
    rows_grad = jnp.dot(sel, grad_ref[...], preferred_element_type=jnp.float32) * scale_ref[:, :1]
    width = send_ref.shape[3] // 2
    for b in range(send_ref.shape[1]):
        cols = slice(b * width, (b + 1) * width)
        both = jnp.concatenate([rows_in[:, cols], rows_grad[:, cols]], axis=1)
        send_ref[:, b] = both.reshape(replicas, PAD, 2 * width).astype(jnp.bfloat16)


def dispatch(tokens, grad_out, route_ids, route_probs, replica_pick, plan, dp_count):
    count, model_width = tokens.shape
    replicas = plan.shape[0]
    width = model_width // dp_count
    top = route_ids.shape[1]
    small = pl.BlockSpec((top, count), lambda i: (0, 0))
    return pl.pallas_call(
        dispatch_kernel,
        grid=(dp_count // 2,),
        in_specs=[
            small,
            small,
            small,
            pl.BlockSpec(memory_space=pltpu.SMEM),
            pl.BlockSpec((count, 2 * width), lambda i: (0, i)),
            pl.BlockSpec((count, 2 * width), lambda i: (0, i)),
        ],
        out_specs=[
            pl.BlockSpec((replicas, 2, PAD, 2 * width), lambda i: (0, i, 0, 0)),
            pl.BlockSpec((replicas * PAD, count), lambda i: (0, 0)),
        ],
        out_shape=[
            jax.ShapeDtypeStruct((replicas, dp_count, PAD, 2 * width), jnp.bfloat16),
            jax.ShapeDtypeStruct((replicas * PAD, count), jnp.bfloat16),
        ],
        scratch_shapes=[pltpu.VMEM((replicas * PAD, 128), jnp.float32)],
        compiler_params=pltpu.CompilerParams(vmem_limit_bytes=32 * 2**20),
        name="dispatch",
    )(route_ids.T, replica_pick.T, route_probs.T, plan, tokens, grad_out)


def combine_kernel(sel_ref, back_ref, out_ref):
    sel = sel_ref[...]
    parts = []
    for b in range(back_ref.shape[1]):
        rows = back_ref[:, b].astype(jnp.float32).reshape(-1, back_ref.shape[3]).astype(jnp.bfloat16)
        parts.append(lax.dot_general(sel, rows, CONTRACT_ROWS, preferred_element_type=jnp.float32))
    out_ref[...] = jnp.concatenate(parts, axis=1).astype(jnp.bfloat16)


def combine(sel, back):
    slots, count = sel.shape
    replicas, dp_count, pad, width = back.shape
    return pl.pallas_call(
        combine_kernel,
        grid=(dp_count // 2,),
        in_specs=[
            pl.BlockSpec((slots, count), lambda i: (0, 0)),
            pl.BlockSpec((replicas, 2, pad, width), lambda i: (0, i, 0, 0)),
        ],
        out_specs=pl.BlockSpec((count, 2 * width), lambda i: (0, i)),
        out_shape=jax.ShapeDtypeStruct((count, dp_count * width), jnp.bfloat16),
        compiler_params=pltpu.CompilerParams(vmem_limit_bytes=32 * 2**20),
        name="combine",
    )(sel, back)


def backward_units(gate, up_val, hidden_grad):
    gate = gate.astype(jnp.float32)
    up_val = up_val.astype(jnp.float32)
    hidden_grad = hidden_grad.astype(jnp.float32)
    sigmoid_gate = jax.nn.sigmoid(gate)
    activated = gate * sigmoid_gate
    hidden = (activated * up_val).astype(jnp.bfloat16)
    up_grad = (hidden_grad * activated).astype(jnp.bfloat16)
    gate_grad = (hidden_grad * up_val * sigmoid_gate * (1.0 + gate * (1.0 - sigmoid_gate))).astype(
        jnp.bfloat16
    )
    return hidden, gate_grad, up_grad


def which_pairing(plan, tables):
    replicas = plan.shape[0]
    same = (plan[:, None] == plan[None, :]) & ~np.eye(replicas, dtype=bool)
    ids = jnp.arange(replicas, dtype=jnp.int32)
    partner = ids + jnp.sum(jnp.where(same, ids[None, :] - ids[:, None], 0), axis=1)
    agree = jnp.all(jnp.asarray(tables, jnp.int32) == partner[None, :], axis=1)
    return jnp.sum(jnp.where(agree, jnp.arange(len(tables), dtype=jnp.int32), 0))


def from_partner(terms, index, tables):
    def branch(partner, value):
        return lax.ppermute(value, "ep", [(r, p) for r, p in enumerate(partner) if p != r])

    return lax.switch(index, [functools.partial(branch, t) for t in tables], terms)


def on_device(tokens, grad_out, route_ids, route_probs, replica_pick, plan, w_gate, w_up, w_down):
    replicas = plan.shape[0]
    dp_count = lax.axis_size("dp")
    width = tokens.shape[1] // dp_count
    tables = pairings(replicas)
    index = which_pairing(plan, tables)
    send, sel = dispatch(tokens, grad_out, route_ids, route_probs, replica_pick, plan, dp_count)
    recv = lax.all_to_all(
        send.reshape(replicas * dp_count, PAD, 2 * width),
        ("ep", "dp"),
        split_axis=0,
        concat_axis=0,
        tiled=True,
    )
    rows = recv[:, :MOST].reshape(-1, 2 * width)
    rows_in, rows_grad = rows[:, :width], rows[:, width:]
    gate_w, up_w, down_w = w_gate[0], w_up[0], w_down[0]
    starts = np.cumsum((0,) + CHUNKS)
    partials = []
    for lo, hi in itertools.pairwise(starts):
        partials.append(
            (
                jnp.dot(rows_in, gate_w[:, lo:hi], preferred_element_type=jnp.float32).astype(jnp.bfloat16),
                jnp.dot(rows_in, up_w[:, lo:hi], preferred_element_type=jnp.float32).astype(jnp.bfloat16),
                lax.dot_general(
                    rows_grad, down_w[lo:hi], CONTRACT_UNITS, preferred_element_type=jnp.float32
                ).astype(jnp.bfloat16),
            )
        )
    row_grads = jnp.float32(0.0)
    finals = []
    summed = lax.psum(partials[0], "dp")
    for c, (lo, hi) in enumerate(itertools.pairwise(starts)):
        if c + 1 < len(CHUNKS):
            summed, following = lax.optimization_barrier((summed, partials[c + 1]))
            following = lax.psum(following, "dp")
        hidden, gate_grad, up_grad = backward_units(*summed)
        terms = jnp.concatenate(
            [
                lax.dot_general(left, right, CONTRACT_ROWS, preferred_element_type=jnp.float32).astype(
                    jnp.bfloat16
                )
                for left, right in ((rows_in, gate_grad), (rows_in, up_grad), (rows_grad, hidden))
            ],
            axis=0,
        )
        row_grads = (
            row_grads
            + lax.dot_general(gate_grad, gate_w[:, lo:hi], CONTRACT_UNITS, preferred_element_type=jnp.float32)
            + lax.dot_general(up_grad, up_w[:, lo:hi], CONTRACT_UNITS, preferred_element_type=jnp.float32)
        )
        other = from_partner(terms, index, tables)
        finals.append((terms.astype(jnp.float32) + other.astype(jnp.float32)).astype(jnp.bfloat16))
        summed = following if c + 1 < len(CHUNKS) else None
    back = row_grads.astype(jnp.bfloat16).reshape(replicas * dp_count, MOST, width)
    back = jnp.pad(back, ((0, 0), (0, PAD - MOST), (0, 0)))
    back = lax.all_to_all(back, ("ep", "dp"), split_axis=0, concat_axis=0, tiled=True)
    grad_tokens = combine(sel, back.reshape(replicas, dp_count, PAD, width))
    grads = jnp.concatenate(finals, axis=1).reshape(3, width, -1)
    return grad_tokens, grads[0][None], grads[1][None], grads[2].T[None]


def solution(mesh):
    return jax.shard_map(
        on_device,
        mesh=mesh,
        in_specs=(
            P(("ep", "dp"), None),
            P(("ep", "dp"), None),
            P(("ep", "dp"), None),
            P(("ep", "dp"), None),
            P(("ep", "dp"), None),
            P(),
            P("ep", "dp", None),
            P("ep", "dp", None),
            P("ep", None, "dp"),
        ),
        out_specs=(
            P(("ep", "dp"), None),
            P("ep", "dp", None),
            P("ep", "dp", None),
            P("ep", None, "dp"),
        ),
        check_vma=False,
    )
```

```python
import functools
import itertools

import jax
import jax.numpy as jnp
import numpy as np
from jax import lax
from jax.experimental import pallas as pl
from jax.experimental.pallas import tpu as pltpu
from jax.sharding import PartitionSpec as P

MOST = 6
PAD = 8
SIDE = 4
CONTRACT_ROWS = (((0,), (0,)), ((), ()))
CONTRACT_UNITS = (((1,), (1,)), ((), ()))


def pairings(replicas):
    tables = []
    pairs = list(itertools.combinations(range(replicas), 2))
    for first, second in itertools.combinations(pairs, 2):
        if not set(first) & set(second):
            partner = list(range(replicas))
            for a, b in (first, second):
                partner[a], partner[b] = b, a
            tables.append(partner)
    return tables


def dispatch_kernel(ids_ref, pick_ref, probs_ref, plan_ref, tok_ref, grad_ref, send_ref, sel_ref, scale_ref):
    replicas = plan_ref.shape[0]
    tokens = ids_ref.shape[1]

    @pl.when(pl.program_id(0) == 0)
    def _():
        ids = ids_ref[...]
        pick = pick_ref[...]
        probs = probs_ref[...]
        hits, weights = [], []
        for r in range(replicas):
            expert = plan_ref[r]
            copies = jnp.int32(0)
            rank = jnp.int32(0)
            for other in range(replicas):
                same = (plan_ref[other] == expert).astype(jnp.int32)
                copies += same
                if other < r:
                    rank += same
            wanted = jnp.where(copies > 1, lax.rem(pick, jnp.int32(2)), 0)
            matched = (ids == expert) & (wanted == rank)
            hits.append(jnp.max(jnp.where(matched, 1.0, 0.0), axis=0, keepdims=True))
            weights.append(jnp.sum(jnp.where(matched, probs, 0.0), axis=0, keepdims=True))
        hit = jnp.concatenate(hits, axis=0)
        earlier = lax.broadcasted_iota(jnp.int32, (tokens, tokens), 0) < lax.broadcasted_iota(
            jnp.int32, (tokens, tokens), 1
        )
        before = jnp.dot(
            hit.astype(jnp.bfloat16),
            earlier.astype(jnp.float32).astype(jnp.bfloat16),
            preferred_element_type=jnp.float32,
        )
        slot = lax.broadcasted_iota(jnp.int32, (PAD, tokens), 0).astype(jnp.float32)
        rows, scales = [], []
        for r in range(replicas):
            chosen = jnp.where((before[r : r + 1] == slot) & (hit[r : r + 1] > 0.0), 1.0, 0.0)
            rows.append(chosen)
            scales.append(jnp.sum(chosen * weights[r], axis=1, keepdims=True))
        sel_ref[...] = jnp.concatenate(rows, axis=0).astype(jnp.bfloat16)
        scale_ref[...] = jnp.broadcast_to(jnp.concatenate(scales, axis=0), scale_ref.shape)

    sel = sel_ref[...]
    rows_in = jnp.dot(sel, tok_ref[...], preferred_element_type=jnp.float32)
    rows_grad = jnp.dot(sel, grad_ref[...], preferred_element_type=jnp.float32) * scale_ref[:, :1]
    width = send_ref.shape[3] // 2
    for b in range(send_ref.shape[1]):
        cols = slice(b * width, (b + 1) * width)
        both = jnp.concatenate([rows_in[:, cols], rows_grad[:, cols]], axis=1)
        send_ref[:, b] = both.reshape(replicas, PAD, 2 * width).astype(jnp.bfloat16)


def dispatch(tokens, grad_out, route_ids, route_probs, replica_pick, plan, dp_count):
    count, model_width = tokens.shape
    replicas = plan.shape[0]
    width = model_width // dp_count
    top = route_ids.shape[1]
    small = pl.BlockSpec((top, count), lambda i: (0, 0))
    return pl.pallas_call(
        dispatch_kernel,
        grid=(dp_count // 2,),
        in_specs=[
            small,
            small,
            small,
            pl.BlockSpec(memory_space=pltpu.SMEM),
            pl.BlockSpec((count, 2 * width), lambda i: (0, i)),
            pl.BlockSpec((count, 2 * width), lambda i: (0, i)),
        ],
        out_specs=[
            pl.BlockSpec((replicas, 2, PAD, 2 * width), lambda i: (0, i, 0, 0)),
            pl.BlockSpec((replicas * PAD, count), lambda i: (0, 0)),
        ],
        out_shape=[
            jax.ShapeDtypeStruct((replicas, dp_count, PAD, 2 * width), jnp.bfloat16),
            jax.ShapeDtypeStruct((replicas * PAD, count), jnp.bfloat16),
        ],
        scratch_shapes=[pltpu.VMEM((replicas * PAD, 128), jnp.float32)],
        compiler_params=pltpu.CompilerParams(vmem_limit_bytes=60 * 2**20),
        name="dispatch",
    )(route_ids.T, replica_pick.T, route_probs.T, plan, tokens, grad_out)


def combine_kernel(sel_ref, back_ref, out_ref):
    sel = sel_ref[...]
    parts = []
    for b in range(back_ref.shape[1]):
        rows = back_ref[:, b].astype(jnp.float32).reshape(-1, back_ref.shape[3]).astype(jnp.bfloat16)
        parts.append(lax.dot_general(sel, rows, CONTRACT_ROWS, preferred_element_type=jnp.float32))
    out_ref[...] = jnp.concatenate(parts, axis=1).astype(jnp.bfloat16)


def combine(sel, back):
    slots, count = sel.shape
    replicas, dp_count, pad, width = back.shape
    return pl.pallas_call(
        combine_kernel,
        grid=(dp_count // 2,),
        in_specs=[
            pl.BlockSpec((slots, count), lambda i: (0, 0)),
            pl.BlockSpec((replicas, 2, pad, width), lambda i: (0, i, 0, 0)),
        ],
        out_specs=pl.BlockSpec((count, 2 * width), lambda i: (0, i)),
        out_shape=jax.ShapeDtypeStruct((count, dp_count * width), jnp.bfloat16),
        compiler_params=pltpu.CompilerParams(vmem_limit_bytes=32 * 2**20),
        name="combine",
    )(sel, back)


def added(first, *others):
    total = first.astype(jnp.float32)
    for other in others:
        total = total + other.astype(jnp.float32)
    return total


def place(axis):
    index = lax.axis_index("dp")
    return index % SIDE if axis == "x" else index // SIDE


def shifted(value, axis, step):
    pairs = []
    for d in range(SIDE * SIDE):
        y, x = divmod(d, SIDE)
        to = y * SIDE + (x + step) % SIDE if axis == "x" else (y + step) % SIDE * SIDE + x
        pairs.append((d, to))
    return lax.ppermute(value, "dp", pairs)


def part_of(value, index):
    return lax.dynamic_index_in_dim(value, index % SIDE, 0, keepdims=False)


def scatter_axis(value, axis):
    here = place(axis)
    half = value.shape[1] // 2
    far = part_of(value, here + 2)
    upward = shifted(far[:half], axis, 1)
    downward = shifted(far[half:], axis, -1)
    right, left = part_of(value, here + 1), part_of(value, here + SIDE - 1)
    right = jnp.concatenate([added(right[:half], upward).astype(jnp.bfloat16), right[half:]], axis=0)
    left = jnp.concatenate([left[:half], added(left[half:], downward).astype(jnp.bfloat16)], axis=0)
    return added(part_of(value, here), shifted(right, axis, 1), shifted(left, axis, -1))


def gather_axis(value, axis):
    here = place(axis)
    half = value.shape[0] // 2
    left, right = shifted(value, axis, 1), shifted(value, axis, -1)
    far = jnp.concatenate([shifted(left[:half], axis, 1), shifted(right[half:], axis, -1)], axis=0)
    out = jnp.zeros((SIDE, *value.shape), value.dtype)
    for offset, piece in enumerate((value, right, far, left)):
        out = lax.dynamic_update_index_in_dim(out, piece, (here + offset) % SIDE, 0)
    return out


def scatter_rows(value, first, second):
    rows, cols = value.shape
    value = scatter_axis(value.reshape(SIDE, rows // SIDE, cols), first).astype(jnp.bfloat16)
    return scatter_axis(value.reshape(SIDE, rows // SIDE**2, cols), second)


def gather_rows(value, first, second):
    cols = value.shape[1]
    value = gather_axis(value, second).reshape(-1, cols)
    return gather_axis(value, first).reshape(-1, cols)


def backward_units(gate, up_val, hidden_grad):
    sigmoid_gate = jax.nn.sigmoid(gate)
    activated = gate * sigmoid_gate
    hidden = (activated * up_val).astype(jnp.bfloat16)
    up_grad = (hidden_grad * activated).astype(jnp.bfloat16)
    gate_grad = (hidden_grad * up_val * sigmoid_gate * (1.0 + gate * (1.0 - sigmoid_gate))).astype(
        jnp.bfloat16
    )
    return hidden, gate_grad, up_grad


def which_pairing(plan, tables):
    replicas = plan.shape[0]
    same = (plan[:, None] == plan[None, :]) & ~np.eye(replicas, dtype=bool)
    ids = jnp.arange(replicas, dtype=jnp.int32)
    partner = ids + jnp.sum(jnp.where(same, ids[None, :] - ids[:, None], 0), axis=1)
    agree = jnp.all(jnp.asarray(tables, jnp.int32) == partner[None, :], axis=1)
    return jnp.sum(jnp.where(agree, jnp.arange(len(tables), dtype=jnp.int32), 0))


def from_partner(terms, index, tables):
    def branch(partner, value):
        return lax.ppermute(value, "ep", [(r, p) for r, p in enumerate(partner) if p != r])

    return lax.switch(index, [functools.partial(branch, t) for t in tables], terms)


def on_device(tokens, grad_out, route_ids, route_probs, replica_pick, plan, w_gate, w_up, w_down):
    replicas = plan.shape[0]
    dp_count = lax.axis_size("dp")
    width = tokens.shape[1] // dp_count
    tables = pairings(replicas)
    index = which_pairing(plan, tables)
    send, sel = dispatch(tokens, grad_out, route_ids, route_probs, replica_pick, plan, dp_count)
    recv = lax.all_to_all(
        send.reshape(replicas * dp_count, PAD, 2 * width),
        ("ep", "dp"),
        split_axis=0,
        concat_axis=0,
        tiled=True,
    )
    rows = recv[:, :MOST].reshape(-1, 2 * width)
    rows_in, rows_grad = rows[:, :width], rows[:, width:]
    gate_w, up_w, down_w = w_gate[0], w_up[0], w_down[0]
    hidden_units = gate_w.shape[1]
    middle = hidden_units // 2
    halves = ((0, middle, ("x", "y")), (middle, hidden_units, ("y", "x")))
    partials = []
    for lo, hi, _ in halves:
        products = (
            jnp.dot(rows_in, gate_w[:, lo:hi], preferred_element_type=jnp.float32),
            jnp.dot(rows_in, up_w[:, lo:hi], preferred_element_type=jnp.float32),
            lax.dot_general(rows_grad, down_w[lo:hi], CONTRACT_UNITS, preferred_element_type=jnp.float32),
        )
        partials.append(jnp.concatenate([p.astype(jnp.bfloat16) for p in products], axis=1))
    row_grads = jnp.float32(0.0)
    terms = []
    for partial, (lo, hi, order) in zip(partials, halves):
        summed = scatter_rows(partial, *order)
        units = backward_units(*jnp.split(summed, 3, axis=1))
        units = gather_rows(jnp.concatenate(units, axis=1), *order)
        hidden, gate_grad, up_grad = jnp.split(units, 3, axis=1)
        terms.append(
            jnp.stack(
                [
                    lax.dot_general(a, b, CONTRACT_ROWS, preferred_element_type=jnp.float32).astype(jnp.bfloat16)
                    for a, b in ((rows_in, gate_grad), (rows_in, up_grad), (rows_grad, hidden))
                ]
            )
        )
        row_grads = (
            row_grads
            + lax.dot_general(gate_grad, gate_w[:, lo:hi], CONTRACT_UNITS, preferred_element_type=jnp.float32)
            + lax.dot_general(up_grad, up_w[:, lo:hi], CONTRACT_UNITS, preferred_element_type=jnp.float32)
        )
    terms = jnp.concatenate(terms, axis=2)
    other = from_partner(terms, index, tables)
    grads = (terms.astype(jnp.float32) + other.astype(jnp.float32)).astype(jnp.bfloat16)
    back = row_grads.astype(jnp.bfloat16).reshape(replicas * dp_count, MOST, width)
    back = jnp.pad(back, ((0, 0), (0, PAD - MOST), (0, 0)))
    back = lax.all_to_all(back, ("ep", "dp"), split_axis=0, concat_axis=0, tiled=True)
    grad_tokens = combine(sel, back.reshape(replicas, dp_count, PAD, width))
    return grad_tokens, grads[0][None], grads[1][None], grads[2].T[None]


def solution(mesh):
    return jax.shard_map(
        on_device,
        mesh=mesh,
        in_specs=(
            P(("ep", "dp"), None),
            P(("ep", "dp"), None),
            P(("ep", "dp"), None),
            P(("ep", "dp"), None),
            P(("ep", "dp"), None),
            P(),
            P("ep", "dp", None),
            P("ep", "dp", None),
            P("ep", None, "dp"),
        ),
        out_specs=(
            P(("ep", "dp"), None),
            P("ep", "dp", None),
            P("ep", "dp", None),
            P("ep", None, "dp"),
        ),
        check_vma=False,
    )
```

```python
import functools
import itertools

import jax
import jax.numpy as jnp
import numpy as np
from jax import lax
from jax.experimental import pallas as pl
from jax.experimental.pallas import tpu as pltpu
from jax.sharding import PartitionSpec as P

MOST = 6
PAD = 8
SIDE = 4
CONTRACT_ROWS = (((0,), (0,)), ((), ()))
CONTRACT_UNITS = (((1,), (1,)), ((), ()))


def pairings(replicas):
    tables = []
    pairs = list(itertools.combinations(range(replicas), 2))
    for first, second in itertools.combinations(pairs, 2):
        if not set(first) & set(second):
            partner = list(range(replicas))
            for a, b in (first, second):
                partner[a], partner[b] = b, a
            tables.append(partner)
    return tables


def dispatch_kernel(ids_ref, pick_ref, probs_ref, plan_ref, tok_ref, grad_ref, send_ref, sel_ref, scale_ref):
    replicas = plan_ref.shape[0]
    tokens = ids_ref.shape[1]

    @pl.when(pl.program_id(0) == 0)
    def _():
        ids = ids_ref[...]
        pick = pick_ref[...]
        probs = probs_ref[...]
        hits, weights = [], []
        for r in range(replicas):
            expert = plan_ref[r]
            copies = jnp.int32(0)
            rank = jnp.int32(0)
            for other in range(replicas):
                same = (plan_ref[other] == expert).astype(jnp.int32)
                copies += same
                if other < r:
                    rank += same
            wanted = jnp.where(copies > 1, lax.rem(pick, jnp.int32(2)), 0)
            matched = (ids == expert) & (wanted == rank)
            hits.append(jnp.max(jnp.where(matched, 1.0, 0.0), axis=0, keepdims=True))
            weights.append(jnp.sum(jnp.where(matched, probs, 0.0), axis=0, keepdims=True))
        hit = jnp.concatenate(hits, axis=0)
        earlier = lax.broadcasted_iota(jnp.int32, (tokens, tokens), 0) < lax.broadcasted_iota(
            jnp.int32, (tokens, tokens), 1
        )
        before = jnp.dot(
            hit.astype(jnp.bfloat16),
            earlier.astype(jnp.float32).astype(jnp.bfloat16),
            preferred_element_type=jnp.float32,
        )
        slot = lax.broadcasted_iota(jnp.int32, (PAD, tokens), 0).astype(jnp.float32)
        rows, scales = [], []
        for r in range(replicas):
            chosen = jnp.where((before[r : r + 1] == slot) & (hit[r : r + 1] > 0.0), 1.0, 0.0)
            rows.append(chosen)
            scales.append(jnp.sum(chosen * weights[r], axis=1, keepdims=True))
        sel_ref[...] = jnp.concatenate(rows, axis=0).astype(jnp.bfloat16)
        scale_ref[...] = jnp.broadcast_to(jnp.concatenate(scales, axis=0), scale_ref.shape)

    sel = sel_ref[...]
    rows_in = jnp.dot(sel, tok_ref[...], preferred_element_type=jnp.float32)
    rows_grad = jnp.dot(sel, grad_ref[...], preferred_element_type=jnp.float32) * scale_ref[:, :1]
    width = send_ref.shape[3] // 2
    for b in range(send_ref.shape[1]):
        cols = slice(b * width, (b + 1) * width)
        both = jnp.concatenate([rows_in[:, cols], rows_grad[:, cols]], axis=1)
        send_ref[:, b] = both.reshape(replicas, PAD, 2 * width).astype(jnp.bfloat16)


def dispatch(tokens, grad_out, route_ids, route_probs, replica_pick, plan, dp_count):
    count, model_width = tokens.shape
    replicas = plan.shape[0]
    width = model_width // dp_count
    top = route_ids.shape[1]
    small = pl.BlockSpec((top, count), lambda i: (0, 0))
    return pl.pallas_call(
        dispatch_kernel,
        grid=(dp_count // 2,),
        in_specs=[
            small,
            small,
            small,
            pl.BlockSpec(memory_space=pltpu.SMEM),
            pl.BlockSpec((count, 2 * width), lambda i: (0, i)),
            pl.BlockSpec((count, 2 * width), lambda i: (0, i)),
        ],
        out_specs=[
            pl.BlockSpec((replicas, 2, PAD, 2 * width), lambda i: (0, i, 0, 0)),
            pl.BlockSpec((replicas * PAD, count), lambda i: (0, 0)),
        ],
        out_shape=[
            jax.ShapeDtypeStruct((replicas, dp_count, PAD, 2 * width), jnp.bfloat16),
            jax.ShapeDtypeStruct((replicas * PAD, count), jnp.bfloat16),
        ],
        scratch_shapes=[pltpu.VMEM((replicas * PAD, 128), jnp.float32)],
        compiler_params=pltpu.CompilerParams(vmem_limit_bytes=60 * 2**20),
        name="dispatch",
    )(route_ids.T, replica_pick.T, route_probs.T, plan, tokens, grad_out)


def combine_kernel(sel_ref, back_ref, out_ref):
    sel = sel_ref[...]
    parts = []
    for b in range(back_ref.shape[1]):
        rows = back_ref[:, b].astype(jnp.float32).reshape(-1, back_ref.shape[3]).astype(jnp.bfloat16)
        parts.append(lax.dot_general(sel, rows, CONTRACT_ROWS, preferred_element_type=jnp.float32))
    out_ref[...] = jnp.concatenate(parts, axis=1).astype(jnp.bfloat16)


def combine(sel, back):
    slots, count = sel.shape
    replicas, dp_count, pad, width = back.shape
    return pl.pallas_call(
        combine_kernel,
        grid=(dp_count // 2,),
        in_specs=[
            pl.BlockSpec((slots, count), lambda i: (0, 0)),
            pl.BlockSpec((replicas, 2, pad, width), lambda i: (0, i, 0, 0)),
        ],
        out_specs=pl.BlockSpec((count, 2 * width), lambda i: (0, i)),
        out_shape=jax.ShapeDtypeStruct((count, dp_count * width), jnp.bfloat16),
        compiler_params=pltpu.CompilerParams(vmem_limit_bytes=32 * 2**20),
        name="combine",
    )(sel, back)


def added(first, *others):
    total = first.astype(jnp.float32)
    for other in others:
        total = total + other.astype(jnp.float32)
    return total


def place(axis):
    index = lax.axis_index("dp")
    return index % SIDE if axis == "x" else index // SIDE


def shifted(value, axis, step):
    pairs = []
    for d in range(SIDE * SIDE):
        y, x = divmod(d, SIDE)
        to = y * SIDE + (x + step) % SIDE if axis == "x" else (y + step) % SIDE * SIDE + x
        pairs.append((d, to))
    return lax.ppermute(value, "dp", pairs)


def part_of(value, index):
    return lax.dynamic_index_in_dim(value, index % SIDE, 0, keepdims=False)


def scatter_axis(value, axis):
    here = place(axis)
    half = value.shape[1] // 2
    far = part_of(value, here + 2)
    upward = shifted(far[:half], axis, 1)
    downward = shifted(far[half:], axis, -1)
    right, left = part_of(value, here + 1), part_of(value, here + SIDE - 1)
    right = jnp.concatenate([added(right[:half], upward).astype(jnp.bfloat16), right[half:]], axis=0)
    left = jnp.concatenate([left[:half], added(left[half:], downward).astype(jnp.bfloat16)], axis=0)
    return added(part_of(value, here), shifted(right, axis, 1), shifted(left, axis, -1))


def gather_axis(value, axis):
    here = place(axis)
    half = value.shape[0] // 2
    left, right = shifted(value, axis, 1), shifted(value, axis, -1)
    far = jnp.concatenate([shifted(left[:half], axis, 1), shifted(right[half:], axis, -1)], axis=0)
    out = jnp.zeros((SIDE, *value.shape), value.dtype)
    for offset, piece in enumerate((value, right, far, left)):
        out = lax.dynamic_update_index_in_dim(out, piece, (here + offset) % SIDE, 0)
    return out


def scatter_rows(value, first, second):
    rows, cols = value.shape
    value = scatter_axis(value.reshape(SIDE, rows // SIDE, cols), first).astype(jnp.bfloat16)
    return scatter_axis(value.reshape(SIDE, rows // SIDE**2, cols), second)


def gather_rows(value, first, second):
    cols = value.shape[1]
    value = gather_axis(value, second).reshape(-1, cols)
    return gather_axis(value, first).reshape(-1, cols)


def backward_units(gate, up_val, hidden_grad):
    sigmoid_gate = jax.nn.sigmoid(gate)
    activated = gate * sigmoid_gate
    hidden = (activated * up_val).astype(jnp.bfloat16)
    up_grad = (hidden_grad * activated).astype(jnp.bfloat16)
    gate_grad = (hidden_grad * up_val * sigmoid_gate * (1.0 + gate * (1.0 - sigmoid_gate))).astype(
        jnp.bfloat16
    )
    return hidden, gate_grad, up_grad


def which_pairing(plan, tables):
    replicas = plan.shape[0]
    same = (plan[:, None] == plan[None, :]) & ~np.eye(replicas, dtype=bool)
    ids = jnp.arange(replicas, dtype=jnp.int32)
    partner = ids + jnp.sum(jnp.where(same, ids[None, :] - ids[:, None], 0), axis=1)
    agree = jnp.all(jnp.asarray(tables, jnp.int32) == partner[None, :], axis=1)
    return jnp.sum(jnp.where(agree, jnp.arange(len(tables), dtype=jnp.int32), 0))


def from_partner(terms, index, tables):
    def branch(partner, value):
        return lax.ppermute(value, "ep", [(r, p) for r, p in enumerate(partner) if p != r])

    return lax.switch(index, [functools.partial(branch, t) for t in tables], terms)


def on_device(tokens, grad_out, route_ids, route_probs, replica_pick, plan, w_gate, w_up, w_down):
    replicas = plan.shape[0]
    dp_count = lax.axis_size("dp")
    width = tokens.shape[1] // dp_count
    tables = pairings(replicas)
    index = which_pairing(plan, tables)
    send, sel = dispatch(tokens, grad_out, route_ids, route_probs, replica_pick, plan, dp_count)
    recv = lax.all_to_all(
        send.reshape(replicas * dp_count, PAD, 2 * width),
        ("ep", "dp"),
        split_axis=0,
        concat_axis=0,
        tiled=True,
    )
    rows = recv[:, :MOST].reshape(-1, 2 * width)
    rows_in, rows_grad = rows[:, :width], rows[:, width:]
    gate_w, up_w, down_w = w_gate[0], w_up[0], w_down[0]
    hidden_units = gate_w.shape[1]
    early = hidden_units // 8 * 3
    middle = early // 2

    def products(lo, hi):
        return [
            p.astype(jnp.bfloat16)
            for p in (
                jnp.dot(rows_in, gate_w[:, lo:hi], preferred_element_type=jnp.float32),
                jnp.dot(rows_in, up_w[:, lo:hi], preferred_element_type=jnp.float32),
                lax.dot_general(rows_grad, down_w[lo:hi], CONTRACT_UNITS, preferred_element_type=jnp.float32),
            )
        ]

    def row_part(gate_grad, up_grad, lo, hi):
        return lax.dot_general(
            gate_grad, gate_w[:, lo:hi], CONTRACT_UNITS, preferred_element_type=jnp.float32
        ) + lax.dot_general(up_grad, up_w[:, lo:hi], CONTRACT_UNITS, preferred_element_type=jnp.float32)

    def replica_terms(hidden, gate_grad, up_grad):
        return jnp.stack(
            [
                lax.dot_general(a, b, CONTRACT_ROWS, preferred_element_type=jnp.float32).astype(jnp.bfloat16)
                for a, b in ((rows_in, gate_grad), (rows_in, up_grad), (rows_grad, hidden))
            ]
        )

    def with_partner(terms):
        return added(terms, from_partner(terms, index, tables)).astype(jnp.bfloat16)

    late = products(early, hidden_units)
    late, rows_in, rows_grad = lax.optimization_barrier((late, rows_in, rows_grad))
    late = lax.psum(late, "dp")
    row_grads = jnp.float32(0.0)
    terms = []
    for lo, hi, order in ((0, middle, ("x", "y")), (middle, early, ("y", "x"))):
        summed = scatter_rows(jnp.concatenate(products(lo, hi), axis=1), *order)
        units = backward_units(*jnp.split(summed, 3, axis=1))
        units = gather_rows(jnp.concatenate(units, axis=1), *order)
        hidden, gate_grad, up_grad = jnp.split(units, 3, axis=1)
        terms.append(replica_terms(hidden, gate_grad, up_grad))
        row_grads = row_grads + row_part(gate_grad, up_grad, lo, hi)
    grads_early = with_partner(jnp.concatenate(terms, axis=2))
    late, grads_early, row_grads = lax.optimization_barrier((late, grads_early, row_grads))
    hidden, gate_grad, up_grad = backward_units(*(part.astype(jnp.float32) for part in late))
    row_grads = row_grads + row_part(gate_grad, up_grad, early, hidden_units)
    grads_late = with_partner(replica_terms(hidden, gate_grad, up_grad))
    grads = jnp.concatenate([grads_early, grads_late], axis=2)
    back = row_grads.astype(jnp.bfloat16).reshape(replicas * dp_count, MOST, width)
    back = jnp.pad(back, ((0, 0), (0, PAD - MOST), (0, 0)))
    back = lax.all_to_all(back, ("ep", "dp"), split_axis=0, concat_axis=0, tiled=True)
    grad_tokens = combine(sel, back.reshape(replicas, dp_count, PAD, width))
    return grad_tokens, grads[0][None], grads[1][None], grads[2].T[None]


def solution(mesh):
    return jax.shard_map(
        on_device,
        mesh=mesh,
        in_specs=(
            P(("ep", "dp"), None),
            P(("ep", "dp"), None),
            P(("ep", "dp"), None),
            P(("ep", "dp"), None),
            P(("ep", "dp"), None),
            P(),
            P("ep", "dp", None),
            P("ep", "dp", None),
            P("ep", None, "dp"),
        ),
        out_specs=(
            P(("ep", "dp"), None),
            P("ep", "dp", None),
            P("ep", "dp", None),
            P("ep", None, "dp"),
        ),
        check_vma=False,
    )
```

```python
import functools
import itertools

import jax
import jax.numpy as jnp
import numpy as np
from jax import lax
from jax.experimental import pallas as pl
from jax.experimental.pallas import tpu as pltpu
from jax.sharding import PartitionSpec as P

MOST = 6
PAD = 8
SIDE = 4
BLOCK = 256
EARLY = 2
CONTRACT_ROWS = (((0,), (0,)), ((), ()))
CONTRACT_UNITS = (((1,), (1,)), ((), ()))


def pairings(replicas):
    tables = []
    pairs = list(itertools.combinations(range(replicas), 2))
    for first, second in itertools.combinations(pairs, 2):
        if not set(first) & set(second):
            partner = list(range(replicas))
            for a, b in (first, second):
                partner[a], partner[b] = b, a
            tables.append(partner)
    return tables


def dispatch_kernel(ids_ref, pick_ref, probs_ref, plan_ref, tok_ref, grad_ref, send_ref, sel_ref, scale_ref):
    replicas = plan_ref.shape[0]
    tokens = ids_ref.shape[1]

    @pl.when(pl.program_id(0) == 0)
    def _():
        ids = ids_ref[...]
        pick = pick_ref[...]
        probs = probs_ref[...]
        hits, weights = [], []
        for r in range(replicas):
            expert = plan_ref[r]
            copies = jnp.int32(0)
            rank = jnp.int32(0)
            for other in range(replicas):
                same = (plan_ref[other] == expert).astype(jnp.int32)
                copies += same
                if other < r:
                    rank += same
            wanted = jnp.where(copies > 1, lax.rem(pick, jnp.int32(2)), 0)
            matched = (ids == expert) & (wanted == rank)
            hits.append(jnp.max(jnp.where(matched, 1.0, 0.0), axis=0, keepdims=True))
            weights.append(jnp.sum(jnp.where(matched, probs, 0.0), axis=0, keepdims=True))
        hit = jnp.concatenate(hits, axis=0)
        earlier = lax.broadcasted_iota(jnp.int32, (tokens, tokens), 0) < lax.broadcasted_iota(
            jnp.int32, (tokens, tokens), 1
        )
        before = jnp.dot(
            hit.astype(jnp.bfloat16),
            earlier.astype(jnp.float32).astype(jnp.bfloat16),
            preferred_element_type=jnp.float32,
        )
        slot = lax.broadcasted_iota(jnp.int32, (PAD, tokens), 0).astype(jnp.float32)
        rows, scales = [], []
        for r in range(replicas):
            chosen = jnp.where((before[r : r + 1] == slot) & (hit[r : r + 1] > 0.0), 1.0, 0.0)
            rows.append(chosen)
            scales.append(jnp.sum(chosen * weights[r], axis=1, keepdims=True))
        sel_ref[...] = jnp.concatenate(rows, axis=0).astype(jnp.bfloat16)
        scale_ref[...] = jnp.broadcast_to(jnp.concatenate(scales, axis=0), scale_ref.shape)

    sel = sel_ref[...]
    rows_in = jnp.dot(sel, tok_ref[...], preferred_element_type=jnp.float32)
    rows_grad = jnp.dot(sel, grad_ref[...], preferred_element_type=jnp.float32) * scale_ref[:, :1]
    width = send_ref.shape[3] // 2
    for b in range(send_ref.shape[1]):
        cols = slice(b * width, (b + 1) * width)
        both = jnp.concatenate([rows_in[:, cols], rows_grad[:, cols]], axis=1)
        send_ref[:, b] = both.reshape(replicas, PAD, 2 * width).astype(jnp.bfloat16)


def dispatch(tokens, grad_out, route_ids, route_probs, replica_pick, plan, dp_count):
    count, model_width = tokens.shape
    replicas = plan.shape[0]
    width = model_width // dp_count
    top = route_ids.shape[1]
    small = pl.BlockSpec((top, count), lambda i: (0, 0))
    return pl.pallas_call(
        dispatch_kernel,
        grid=(dp_count // 2,),
        in_specs=[
            small,
            small,
            small,
            pl.BlockSpec(memory_space=pltpu.SMEM),
            pl.BlockSpec((count, 2 * width), lambda i: (0, i)),
            pl.BlockSpec((count, 2 * width), lambda i: (0, i)),
        ],
        out_specs=[
            pl.BlockSpec((replicas, 2, PAD, 2 * width), lambda i: (0, i, 0, 0)),
            pl.BlockSpec((replicas * PAD, count), lambda i: (0, 0)),
        ],
        out_shape=[
            jax.ShapeDtypeStruct((replicas, dp_count, PAD, 2 * width), jnp.bfloat16),
            jax.ShapeDtypeStruct((replicas * PAD, count), jnp.bfloat16),
        ],
        scratch_shapes=[pltpu.VMEM((replicas * PAD, 128), jnp.float32)],
        compiler_params=pltpu.CompilerParams(vmem_limit_bytes=60 * 2**20),
        name="dispatch",
    )(route_ids.T, replica_pick.T, route_probs.T, plan, tokens, grad_out)


def combine_kernel(sel_ref, back_ref, out_ref):
    sel = sel_ref[...]
    parts = []
    for b in range(back_ref.shape[1]):
        rows = back_ref[:, b].astype(jnp.float32).reshape(-1, back_ref.shape[3]).astype(jnp.bfloat16)
        parts.append(lax.dot_general(sel, rows, CONTRACT_ROWS, preferred_element_type=jnp.float32))
    out_ref[...] = jnp.concatenate(parts, axis=1).astype(jnp.bfloat16)


def combine(sel, back):
    slots, count = sel.shape
    replicas, dp_count, pad, width = back.shape
    return pl.pallas_call(
        combine_kernel,
        grid=(dp_count // 2,),
        in_specs=[
            pl.BlockSpec((slots, count), lambda i: (0, 0)),
            pl.BlockSpec((replicas, 2, pad, width), lambda i: (0, i, 0, 0)),
        ],
        out_specs=pl.BlockSpec((count, 2 * width), lambda i: (0, i)),
        out_shape=jax.ShapeDtypeStruct((count, dp_count * width), jnp.bfloat16),
        compiler_params=pltpu.CompilerParams(vmem_limit_bytes=32 * 2**20),
        name="combine",
    )(sel, back)


def added(first, *others):
    total = first.astype(jnp.float32)
    for other in others:
        total = total + other.astype(jnp.float32)
    return total


def place(axis):
    index = lax.axis_index("dp")
    return index % SIDE if axis == "x" else index // SIDE


def shifted(value, axis, step):
    pairs = []
    for d in range(SIDE * SIDE):
        y, x = divmod(d, SIDE)
        to = y * SIDE + (x + step) % SIDE if axis == "x" else (y + step) % SIDE * SIDE + x
        pairs.append((d, to))
    return lax.ppermute(value, "dp", pairs)


def part_of(value, index):
    return lax.dynamic_index_in_dim(value, index % SIDE, 0, keepdims=False)


def scatter_axis(value, axis):
    here = place(axis)
    half = value.shape[1] // 2
    far = part_of(value, here + 2)
    upward = shifted(far[:half], axis, 1)
    downward = shifted(far[half:], axis, -1)
    right, left = part_of(value, here + 1), part_of(value, here + SIDE - 1)
    right = jnp.concatenate([added(right[:half], upward).astype(jnp.bfloat16), right[half:]], axis=0)
    left = jnp.concatenate([left[:half], added(left[half:], downward).astype(jnp.bfloat16)], axis=0)
    return added(part_of(value, here), shifted(right, axis, 1), shifted(left, axis, -1))


def gather_axis(value, axis):
    here = place(axis)
    half = value.shape[0] // 2
    left, right = shifted(value, axis, 1), shifted(value, axis, -1)
    far = jnp.concatenate([shifted(left[:half], axis, 1), shifted(right[half:], axis, -1)], axis=0)
    out = jnp.zeros((SIDE, *value.shape), value.dtype)
    for offset, piece in enumerate((value, right, far, left)):
        out = lax.dynamic_update_index_in_dim(out, piece, (here + offset) % SIDE, 0)
    return out


def scatter_rows(value, first, second):
    rows, cols = value.shape
    value = scatter_axis(value.reshape(SIDE, rows // SIDE, cols), first).astype(jnp.bfloat16)
    return scatter_axis(value.reshape(SIDE, rows // SIDE**2, cols), second)


def gather_rows(value, first, second):
    cols = value.shape[1]
    value = gather_axis(value, second).reshape(-1, cols)
    return gather_axis(value, first).reshape(-1, cols)


def backward_units(gate, up_val, hidden_grad):
    sigmoid_gate = jax.nn.sigmoid(gate)
    activated = gate * sigmoid_gate
    hidden = (activated * up_val).astype(jnp.bfloat16)
    up_grad = (hidden_grad * activated).astype(jnp.bfloat16)
    gate_grad = (hidden_grad * up_val * sigmoid_gate * (1.0 + gate * (1.0 - sigmoid_gate))).astype(
        jnp.bfloat16
    )
    return hidden, gate_grad, up_grad


def products_kernel(early, in_ref, grad_ref, gate_ref, up_ref, down_ref, late_ref, early_ref):
    step = pl.program_id(0)
    late = pl.num_programs(0) - early
    width = gate_ref.shape[1]
    for k, (rows, weight) in enumerate(((in_ref, gate_ref), (in_ref, up_ref), (grad_ref, down_ref))):
        product = jnp.dot(rows[...], weight[...], preferred_element_type=jnp.float32).astype(jnp.bfloat16)

        @pl.when(step < late)
        def _():
            late_ref[k] = product

        @pl.when(step >= late)
        def _():
            early_ref[0, :, k * width : (k + 1) * width] = product


def products(rows_in, rows_grad, gate_w, up_w, down_t, early):
    rows, width = rows_in.shape
    blocks = gate_w.shape[1] // BLOCK
    late = blocks - early
    whole = pl.BlockSpec((rows, width), lambda i: (0, 0))
    weight = pl.BlockSpec((width, BLOCK), lambda i: (0, lax.rem(i + early, blocks)))
    return pl.pallas_call(
        functools.partial(products_kernel, early),
        grid=(blocks,),
        in_specs=[whole, whole, weight, weight, weight],
        out_specs=[
            pl.BlockSpec((3, rows, BLOCK), lambda i: (0, 0, jnp.minimum(i, late - 1))),
            pl.BlockSpec((1, rows, 3 * BLOCK), lambda i: (jnp.maximum(i - late, 0), 0, 0)),
        ],
        out_shape=[
            jax.ShapeDtypeStruct((3, rows, late * BLOCK), jnp.bfloat16),
            jax.ShapeDtypeStruct((early, rows, 3 * BLOCK), jnp.bfloat16),
        ],
        compiler_params=pltpu.CompilerParams(vmem_limit_bytes=60 * 2**20),
        cost_estimate=pl.CostEstimate(
            flops=6 * rows * width * blocks * BLOCK, bytes_accessed=20 * 2**20, transcendentals=0
        ),
        name="products",
    )(rows_in, rows_grad, gate_w, up_w, down_t)


def units_kernel(in_ref, grad_ref, sums_ref, gate_ref, up_ref, start_ref, terms_ref, rows_ref, total_ref):
    step = pl.program_id(0)
    hidden, gate_grad, up_grad = backward_units(*(sums_ref[k].astype(jnp.float32) for k in range(3)))
    for k, (rows, units) in enumerate(((in_ref, gate_grad), (in_ref, up_grad), (grad_ref, hidden))):
        terms_ref[k] = jnp.dot(rows[...], units, preferred_element_type=jnp.float32).astype(jnp.bfloat16)
    part = lax.dot_general(
        gate_grad, gate_ref[...], CONTRACT_UNITS, preferred_element_type=jnp.float32
    ) + lax.dot_general(up_grad, up_ref[...], CONTRACT_UNITS, preferred_element_type=jnp.float32)

    @pl.when(step == 0)
    def _():
        total_ref[...] = start_ref[...] + part

    @pl.when(step > 0)
    def _():
        total_ref[...] += part

    @pl.when(step == pl.num_programs(0) - 1)
    def _():
        rows_ref[...] = total_ref[...].astype(jnp.bfloat16)


def late_units(in_t, grad_t, sums, gate_w, up_w, start, early):
    width, rows = in_t.shape
    count = sums.shape[2]
    blocks = count // BLOCK
    whole = pl.BlockSpec((width, rows), lambda i: (0, 0))
    weight = pl.BlockSpec((width, BLOCK), lambda i: (0, i + early))
    return pl.pallas_call(
        units_kernel,
        grid=(blocks,),
        in_specs=[
            whole,
            whole,
            pl.BlockSpec((3, rows, BLOCK), lambda i: (0, 0, i)),
            weight,
            weight,
            pl.BlockSpec((rows, width), lambda i: (0, 0)),
        ],
        out_specs=[
            pl.BlockSpec((3, width, BLOCK), lambda i: (0, 0, i)),
            pl.BlockSpec((rows, width), lambda i: (0, 0)),
        ],
        out_shape=[
            jax.ShapeDtypeStruct((3, width, count), jnp.bfloat16),
            jax.ShapeDtypeStruct((rows, width), jnp.bfloat16),
        ],
        scratch_shapes=[pltpu.VMEM((rows, width), jnp.float32)],
        compiler_params=pltpu.CompilerParams(vmem_limit_bytes=60 * 2**20),
        cost_estimate=pl.CostEstimate(
            flops=10 * rows * width * count, bytes_accessed=20 * 2**20, transcendentals=rows * count
        ),
        name="late_units",
    )(in_t, grad_t, sums, gate_w, up_w, start)


def which_pairing(plan, tables):
    replicas = plan.shape[0]
    same = (plan[:, None] == plan[None, :]) & ~np.eye(replicas, dtype=bool)
    ids = jnp.arange(replicas, dtype=jnp.int32)
    partner = ids + jnp.sum(jnp.where(same, ids[None, :] - ids[:, None], 0), axis=1)
    agree = jnp.all(jnp.asarray(tables, jnp.int32) == partner[None, :], axis=1)
    return jnp.sum(jnp.where(agree, jnp.arange(len(tables), dtype=jnp.int32), 0))


def from_partner(terms, index, tables):
    def branch(partner, value):
        return lax.ppermute(value, "ep", [(r, p) for r, p in enumerate(partner) if p != r])

    return lax.switch(index, [functools.partial(branch, t) for t in tables], terms)


def on_device(tokens, grad_out, route_ids, route_probs, replica_pick, plan, w_gate, w_up, w_down):
    replicas = plan.shape[0]
    dp_count = lax.axis_size("dp")
    width = tokens.shape[1] // dp_count
    tables = pairings(replicas)
    index = which_pairing(plan, tables)
    send, sel = dispatch(tokens, grad_out, route_ids, route_probs, replica_pick, plan, dp_count)
    recv = lax.all_to_all(
        send.reshape(replicas * dp_count, PAD, 2 * width),
        ("ep", "dp"),
        split_axis=0,
        concat_axis=0,
        tiled=True,
    )
    rows_in = recv[:, :MOST, :width].reshape(-1, width)
    rows_grad = recv[:, :MOST, width:].reshape(-1, width)
    gate_w, up_w, down_t = w_gate[0], w_up[0], w_down[0].T
    late, first = products(rows_in, rows_grad, gate_w, up_w, down_t, EARLY)
    late = lax.psum(late, "dp")
    row_grads = jnp.float32(0.0)
    terms = []
    for c in range(EARLY):
        order = ("x", "y") if c % 2 == 0 else ("y", "x")
        here = slice(c * BLOCK, (c + 1) * BLOCK)
        summed = scatter_rows(first[c], *order)
        units = backward_units(*jnp.split(summed, 3, axis=1))
        units = gather_rows(jnp.concatenate(units, axis=1), *order)
        hidden, gate_grad, up_grad = jnp.split(units, 3, axis=1)
        terms.append(
            jnp.stack(
                [
                    lax.dot_general(a, b, CONTRACT_ROWS, preferred_element_type=jnp.float32).astype(jnp.bfloat16)
                    for a, b in ((rows_in, gate_grad), (rows_in, up_grad), (rows_grad, hidden))
                ]
            )
        )
        row_grads = (
            row_grads
            + lax.dot_general(gate_grad, gate_w[:, here], CONTRACT_UNITS, preferred_element_type=jnp.float32)
            + lax.dot_general(up_grad, up_w[:, here], CONTRACT_UNITS, preferred_element_type=jnp.float32)
        )

    def with_partner(terms):
        return added(terms, from_partner(terms, index, tables)).astype(jnp.bfloat16)

    grads_early = with_partner(jnp.concatenate(terms, axis=2))
    in_t, grad_t = rows_in.T, rows_grad.T
    late, grads_early, row_grads, in_t, grad_t = lax.optimization_barrier(
        (late, grads_early, row_grads, in_t, grad_t)
    )
    terms, row_grads = late_units(in_t, grad_t, late, gate_w, up_w, row_grads, EARLY)
    grads_late = with_partner(terms)
    grads = jnp.concatenate([grads_early, grads_late], axis=2)
    back = row_grads.reshape(replicas * dp_count, MOST, width)
    back = jnp.pad(back, ((0, 0), (0, PAD - MOST), (0, 0)))
    back = lax.all_to_all(back, ("ep", "dp"), split_axis=0, concat_axis=0, tiled=True)
    grad_tokens = combine(sel, back.reshape(replicas, dp_count, PAD, width))
    return grad_tokens, grads[0][None], grads[1][None], grads[2].T[None]


def solution(mesh):
    return jax.shard_map(
        on_device,
        mesh=mesh,
        in_specs=(
            P(("ep", "dp"), None),
            P(("ep", "dp"), None),
            P(("ep", "dp"), None),
            P(("ep", "dp"), None),
            P(("ep", "dp"), None),
            P(),
            P("ep", "dp", None),
            P("ep", "dp", None),
            P("ep", None, "dp"),
        ),
        out_specs=(
            P(("ep", "dp"), None),
            P("ep", "dp", None),
            P("ep", "dp", None),
            P("ep", None, "dp"),
        ),
        check_vma=False,
    )
```

```python
import functools
import itertools

import jax
import jax.numpy as jnp
import numpy as np
from jax import lax
from jax.experimental import pallas as pl
from jax.experimental.pallas import tpu as pltpu
from jax.sharding import PartitionSpec as P

MOST = 6
PAD = 8
BLOCK = 256
CONTRACT_ROWS = (((0,), (0,)), ((), ()))
CONTRACT_UNITS = (((1,), (1,)), ((), ()))


def pairings(replicas):
    tables = []
    pairs = list(itertools.combinations(range(replicas), 2))
    for first, second in itertools.combinations(pairs, 2):
        if not set(first) & set(second):
            partner = list(range(replicas))
            for a, b in (first, second):
                partner[a], partner[b] = b, a
            tables.append(partner)
    return tables


def dispatch_kernel(ids_ref, pick_ref, probs_ref, plan_ref, tok_ref, grad_ref, send_ref, sel_ref, scale_ref):
    replicas = plan_ref.shape[0]
    tokens = ids_ref.shape[1]

    @pl.when(pl.program_id(0) == 0)
    def _():
        ids = ids_ref[...]
        pick = pick_ref[...]
        probs = probs_ref[...]
        hits, weights = [], []
        for r in range(replicas):
            expert = plan_ref[r]
            copies = jnp.int32(0)
            rank = jnp.int32(0)
            for other in range(replicas):
                same = (plan_ref[other] == expert).astype(jnp.int32)
                copies += same
                if other < r:
                    rank += same
            wanted = jnp.where(copies > 1, lax.rem(pick, jnp.int32(2)), 0)
            matched = (ids == expert) & (wanted == rank)
            hits.append(jnp.max(jnp.where(matched, 1.0, 0.0), axis=0, keepdims=True))
            weights.append(jnp.sum(jnp.where(matched, probs, 0.0), axis=0, keepdims=True))
        hit = jnp.concatenate(hits, axis=0)
        earlier = lax.broadcasted_iota(jnp.int32, (tokens, tokens), 0) < lax.broadcasted_iota(
            jnp.int32, (tokens, tokens), 1
        )
        before = jnp.dot(
            hit.astype(jnp.bfloat16),
            earlier.astype(jnp.float32).astype(jnp.bfloat16),
            preferred_element_type=jnp.float32,
        )
        slot = lax.broadcasted_iota(jnp.int32, (PAD, tokens), 0).astype(jnp.float32)
        rows, scales = [], []
        for r in range(replicas):
            chosen = jnp.where((before[r : r + 1] == slot) & (hit[r : r + 1] > 0.0), 1.0, 0.0)
            rows.append(chosen)
            scales.append(jnp.sum(chosen * weights[r], axis=1, keepdims=True))
        sel_ref[...] = jnp.concatenate(rows, axis=0).astype(jnp.bfloat16)
        scale_ref[...] = jnp.broadcast_to(jnp.concatenate(scales, axis=0), scale_ref.shape)

    sel = sel_ref[...]
    rows_in = jnp.dot(sel, tok_ref[...], preferred_element_type=jnp.float32)
    rows_grad = jnp.dot(sel, grad_ref[...], preferred_element_type=jnp.float32) * scale_ref[:, :1]
    width = send_ref.shape[3] // 2
    for b in range(send_ref.shape[1]):
        cols = slice(b * width, (b + 1) * width)
        both = jnp.concatenate([rows_in[:, cols], rows_grad[:, cols]], axis=1)
        send_ref[:, b] = both.reshape(replicas, PAD, 2 * width).astype(jnp.bfloat16)


def dispatch(tokens, grad_out, route_ids, route_probs, replica_pick, plan, dp_count):
    count, model_width = tokens.shape
    replicas = plan.shape[0]
    width = model_width // dp_count
    top = route_ids.shape[1]
    small = pl.BlockSpec((top, count), lambda i: (0, 0))
    return pl.pallas_call(
        dispatch_kernel,
        grid=(dp_count // 2,),
        in_specs=[
            small,
            small,
            small,
            pl.BlockSpec(memory_space=pltpu.SMEM),
            pl.BlockSpec((count, 2 * width), lambda i: (0, i)),
            pl.BlockSpec((count, 2 * width), lambda i: (0, i)),
        ],
        out_specs=[
            pl.BlockSpec((replicas, 2, PAD, 2 * width), lambda i: (0, i, 0, 0)),
            pl.BlockSpec((replicas * PAD, count), lambda i: (0, 0)),
        ],
        out_shape=[
            jax.ShapeDtypeStruct((replicas, dp_count, PAD, 2 * width), jnp.bfloat16),
            jax.ShapeDtypeStruct((replicas * PAD, count), jnp.bfloat16),
        ],
        scratch_shapes=[pltpu.VMEM((replicas * PAD, 128), jnp.float32)],
        compiler_params=pltpu.CompilerParams(vmem_limit_bytes=60 * 2**20),
        name="dispatch",
    )(route_ids.T, replica_pick.T, route_probs.T, plan, tokens, grad_out)


def combine_kernel(sel_ref, back_ref, out_ref):
    sel = sel_ref[...]
    parts = []
    for b in range(back_ref.shape[1]):
        rows = back_ref[:, b].astype(jnp.float32).reshape(-1, back_ref.shape[3]).astype(jnp.bfloat16)
        parts.append(lax.dot_general(sel, rows, CONTRACT_ROWS, preferred_element_type=jnp.float32))
    out_ref[...] = jnp.concatenate(parts, axis=1).astype(jnp.bfloat16)


def combine(sel, back):
    slots, count = sel.shape
    replicas, dp_count, pad, width = back.shape
    return pl.pallas_call(
        combine_kernel,
        grid=(dp_count // 2,),
        in_specs=[
            pl.BlockSpec((slots, count), lambda i: (0, 0)),
            pl.BlockSpec((replicas, 2, pad, width), lambda i: (0, i, 0, 0)),
        ],
        out_specs=pl.BlockSpec((count, 2 * width), lambda i: (0, i)),
        out_shape=jax.ShapeDtypeStruct((count, dp_count * width), jnp.bfloat16),
        compiler_params=pltpu.CompilerParams(vmem_limit_bytes=32 * 2**20),
        name="combine",
    )(sel, back)


def added(first, *others):
    total = first.astype(jnp.float32)
    for other in others:
        total = total + other.astype(jnp.float32)
    return total


def backward_units(gate, up_val, hidden_grad):
    sigmoid_gate = jax.nn.sigmoid(gate)
    activated = gate * sigmoid_gate
    hidden = (activated * up_val).astype(jnp.bfloat16)
    up_grad = (hidden_grad * activated).astype(jnp.bfloat16)
    gate_grad = (hidden_grad * up_val * sigmoid_gate * (1.0 + gate * (1.0 - sigmoid_gate))).astype(
        jnp.bfloat16
    )
    return hidden, gate_grad, up_grad


def units_kernel(in_ref, grad_ref, gate_sum, up_sum, down_sum, gate_ref, up_ref, terms_ref, rows_ref, total_ref):
    step = pl.program_id(0)
    hidden, gate_grad, up_grad = backward_units(
        *(part[...].astype(jnp.float32) for part in (gate_sum, up_sum, down_sum))
    )
    for k, (rows, units) in enumerate(((in_ref, gate_grad), (in_ref, up_grad), (grad_ref, hidden))):
        terms_ref[k] = jnp.dot(rows[...], units, preferred_element_type=jnp.float32).astype(jnp.bfloat16)
    part = lax.dot_general(
        gate_grad, gate_ref[...], CONTRACT_UNITS, preferred_element_type=jnp.float32
    ) + lax.dot_general(up_grad, up_ref[...], CONTRACT_UNITS, preferred_element_type=jnp.float32)

    @pl.when(step == 0)
    def _():
        total_ref[...] = part

    @pl.when(step > 0)
    def _():
        total_ref[...] += part

    @pl.when(step == pl.num_programs(0) - 1)
    def _():
        rows_ref[...] = total_ref[...].astype(jnp.bfloat16)


def unit_terms(in_t, grad_t, sums, gate_w, up_w):
    width, rows = in_t.shape
    count = gate_w.shape[1]
    whole = pl.BlockSpec((width, rows), lambda i: (0, 0))
    part = pl.BlockSpec((rows, BLOCK), lambda i: (0, i))
    weight = pl.BlockSpec((width, BLOCK), lambda i: (0, i))
    return pl.pallas_call(
        units_kernel,
        grid=(count // BLOCK,),
        in_specs=[whole, whole, part, part, part, weight, weight],
        out_specs=[
            pl.BlockSpec((3, width, BLOCK), lambda i: (0, 0, i)),
            pl.BlockSpec((rows, width), lambda i: (0, 0)),
        ],
        out_shape=[
            jax.ShapeDtypeStruct((3, width, count), jnp.bfloat16),
            jax.ShapeDtypeStruct((rows, width), jnp.bfloat16),
        ],
        scratch_shapes=[pltpu.VMEM((rows, width), jnp.float32)],
        compiler_params=pltpu.CompilerParams(vmem_limit_bytes=60 * 2**20),
        cost_estimate=pl.CostEstimate(
            flops=10 * rows * width * count, bytes_accessed=20 * 2**20, transcendentals=rows * count
        ),
        name="unit_terms",
    )(in_t, grad_t, *sums, gate_w, up_w)


def which_pairing(plan, tables):
    replicas = plan.shape[0]
    same = (plan[:, None] == plan[None, :]) & ~np.eye(replicas, dtype=bool)
    ids = jnp.arange(replicas, dtype=jnp.int32)
    partner = ids + jnp.sum(jnp.where(same, ids[None, :] - ids[:, None], 0), axis=1)
    agree = jnp.all(jnp.asarray(tables, jnp.int32) == partner[None, :], axis=1)
    return jnp.sum(jnp.where(agree, jnp.arange(len(tables), dtype=jnp.int32), 0))


def from_partner(terms, index, tables):
    def branch(partner, value):
        return lax.ppermute(value, "ep", [(r, p) for r, p in enumerate(partner) if p != r])

    return lax.switch(index, [functools.partial(branch, t) for t in tables], terms)


def on_device(tokens, grad_out, route_ids, route_probs, replica_pick, plan, w_gate, w_up, w_down):
    replicas = plan.shape[0]
    dp_count = lax.axis_size("dp")
    width = tokens.shape[1] // dp_count
    tables = pairings(replicas)
    index = which_pairing(plan, tables)
    send, sel = dispatch(tokens, grad_out, route_ids, route_probs, replica_pick, plan, dp_count)
    recv = lax.all_to_all(
        send.reshape(replicas * dp_count, PAD, 2 * width),
        ("ep", "dp"),
        split_axis=0,
        concat_axis=0,
        tiled=True,
    )
    rows = recv[:, :MOST].reshape(-1, 2 * width)
    rows_in, rows_grad = rows[:, :width], rows[:, width:]
    gate_w, up_w, down_w = w_gate[0], w_up[0], w_down[0]
    sums = lax.psum(
        tuple(
            p.astype(jnp.bfloat16)
            for p in (
                jnp.dot(rows_in, gate_w, preferred_element_type=jnp.float32),
                jnp.dot(rows_in, up_w, preferred_element_type=jnp.float32),
                lax.dot_general(rows_grad, down_w, CONTRACT_UNITS, preferred_element_type=jnp.float32),
            )
        ),
        "dp",
    )
    in_t, grad_t, index, sums = lax.optimization_barrier((rows_in.T, rows_grad.T, index, sums))
    terms, row_grads = unit_terms(in_t, grad_t, sums, gate_w, up_w)
    other = from_partner(terms, index, tables)
    grads = [added(terms[k], other[k]).astype(jnp.bfloat16) for k in range(3)]
    back = row_grads.reshape(replicas * dp_count, MOST, width)
    back = jnp.pad(back, ((0, 0), (0, PAD - MOST), (0, 0)))
    back = lax.all_to_all(back, ("ep", "dp"), split_axis=0, concat_axis=0, tiled=True)
    grad_tokens = combine(sel, back.reshape(replicas, dp_count, PAD, width))
    return grad_tokens, grads[0][None], grads[1][None], grads[2].T[None]


def solution(mesh):
    return jax.shard_map(
        on_device,
        mesh=mesh,
        in_specs=(
            P(("ep", "dp"), None),
            P(("ep", "dp"), None),
            P(("ep", "dp"), None),
            P(("ep", "dp"), None),
            P(("ep", "dp"), None),
            P(),
            P("ep", "dp", None),
            P("ep", "dp", None),
            P("ep", None, "dp"),
        ),
        out_specs=(
            P(("ep", "dp"), None),
            P("ep", "dp", None),
            P("ep", "dp", None),
            P("ep", None, "dp"),
        ),
        check_vma=False,
    )
```

```python
import functools
import itertools

import jax
import jax.numpy as jnp
import numpy as np
from jax import lax
from jax.experimental import pallas as pl
from jax.experimental.pallas import tpu as pltpu
from jax.sharding import PartitionSpec as P

MOST = 6
PAD = 8
BLOCK = 256
CORES = 2
CONTRACT_ROWS = (((0,), (0,)), ((), ()))
CONTRACT_UNITS = (((1,), (1,)), ((), ()))


def pairings(replicas):
    tables = []
    pairs = list(itertools.combinations(range(replicas), 2))
    for first, second in itertools.combinations(pairs, 2):
        if not set(first) & set(second):
            partner = list(range(replicas))
            for a, b in (first, second):
                partner[a], partner[b] = b, a
            tables.append(partner)
    return tables


def dispatch_kernel(ids_ref, pick_ref, probs_ref, plan_ref, tok_ref, grad_ref, send_ref, sel_ref, scale_ref):
    replicas = plan_ref.shape[0]
    tokens = ids_ref.shape[1]

    @pl.when(pl.program_id(0) == 0)
    def _():
        ids = ids_ref[...]
        pick = pick_ref[...]
        probs = probs_ref[...]
        hits, weights = [], []
        for r in range(replicas):
            expert = plan_ref[r]
            copies = jnp.int32(0)
            rank = jnp.int32(0)
            for other in range(replicas):
                same = (plan_ref[other] == expert).astype(jnp.int32)
                copies += same
                if other < r:
                    rank += same
            wanted = jnp.where(copies > 1, lax.rem(pick, jnp.int32(2)), 0)
            matched = (ids == expert) & (wanted == rank)
            hits.append(jnp.max(jnp.where(matched, 1.0, 0.0), axis=0, keepdims=True))
            weights.append(jnp.sum(jnp.where(matched, probs, 0.0), axis=0, keepdims=True))
        hit = jnp.concatenate(hits, axis=0)
        earlier = lax.broadcasted_iota(jnp.int32, (tokens, tokens), 0) < lax.broadcasted_iota(
            jnp.int32, (tokens, tokens), 1
        )
        before = jnp.dot(
            hit.astype(jnp.bfloat16),
            earlier.astype(jnp.float32).astype(jnp.bfloat16),
            preferred_element_type=jnp.float32,
        )
        slot = lax.broadcasted_iota(jnp.int32, (PAD, tokens), 0).astype(jnp.float32)
        rows, scales = [], []
        for r in range(replicas):
            chosen = jnp.where((before[r : r + 1] == slot) & (hit[r : r + 1] > 0.0), 1.0, 0.0)
            rows.append(chosen)
            scales.append(jnp.sum(chosen * weights[r], axis=1, keepdims=True))
        sel_ref[...] = jnp.concatenate(rows, axis=0).astype(jnp.bfloat16)
        scale_ref[...] = jnp.broadcast_to(jnp.concatenate(scales, axis=0), scale_ref.shape)

    sel = sel_ref[...]
    rows_in = jnp.dot(sel, tok_ref[...], preferred_element_type=jnp.float32)
    rows_grad = jnp.dot(sel, grad_ref[...], preferred_element_type=jnp.float32) * scale_ref[:, :1]
    width = send_ref.shape[3] // 2
    for b in range(send_ref.shape[1]):
        cols = slice(b * width, (b + 1) * width)
        both = jnp.concatenate([rows_in[:, cols], rows_grad[:, cols]], axis=1)
        send_ref[:, b] = both.reshape(replicas, PAD, 2 * width).astype(jnp.bfloat16)


def dispatch(tokens, grad_out, route_ids, route_probs, replica_pick, plan, dp_count):
    count, model_width = tokens.shape
    replicas = plan.shape[0]
    width = model_width // dp_count
    top = route_ids.shape[1]
    small = pl.BlockSpec((top, count), lambda i: (0, 0))
    return pl.pallas_call(
        dispatch_kernel,
        grid=(dp_count // 2,),
        in_specs=[
            small,
            small,
            small,
            pl.BlockSpec(memory_space=pltpu.SMEM),
            pl.BlockSpec((count, 2 * width), lambda i: (0, i)),
            pl.BlockSpec((count, 2 * width), lambda i: (0, i)),
        ],
        out_specs=[
            pl.BlockSpec((replicas, 2, PAD, 2 * width), lambda i: (0, i, 0, 0)),
            pl.BlockSpec((replicas * PAD, count), lambda i: (0, 0)),
        ],
        out_shape=[
            jax.ShapeDtypeStruct((replicas, dp_count, PAD, 2 * width), jnp.bfloat16),
            jax.ShapeDtypeStruct((replicas * PAD, count), jnp.bfloat16),
        ],
        scratch_shapes=[pltpu.VMEM((replicas * PAD, 128), jnp.float32)],
        compiler_params=pltpu.CompilerParams(vmem_limit_bytes=60 * 2**20),
        name="dispatch",
    )(route_ids.T, replica_pick.T, route_probs.T, plan, tokens, grad_out)


def combine_kernel(sel_ref, back_ref, out_ref):
    sel = sel_ref[...]
    parts = []
    for b in range(back_ref.shape[1]):
        rows = back_ref[:, b].astype(jnp.float32).reshape(-1, back_ref.shape[3]).astype(jnp.bfloat16)
        parts.append(lax.dot_general(sel, rows, CONTRACT_ROWS, preferred_element_type=jnp.float32))
    out_ref[...] = jnp.concatenate(parts, axis=1).astype(jnp.bfloat16)


def combine(sel, back):
    slots, count = sel.shape
    replicas, dp_count, pad, width = back.shape
    return pl.pallas_call(
        combine_kernel,
        grid=(dp_count // 2,),
        in_specs=[
            pl.BlockSpec((slots, count), lambda i: (0, 0)),
            pl.BlockSpec((replicas, 2, pad, width), lambda i: (0, i, 0, 0)),
        ],
        out_specs=pl.BlockSpec((count, 2 * width), lambda i: (0, i)),
        out_shape=jax.ShapeDtypeStruct((count, dp_count * width), jnp.bfloat16),
        compiler_params=pltpu.CompilerParams(vmem_limit_bytes=32 * 2**20),
        name="combine",
    )(sel, back)


def added(first, *others):
    total = first.astype(jnp.float32)
    for other in others:
        total = total + other.astype(jnp.float32)
    return total


def backward_units(gate, up_val, hidden_grad):
    sigmoid_gate = jax.nn.sigmoid(gate)
    activated = gate * sigmoid_gate
    hidden = (activated * up_val).astype(jnp.bfloat16)
    up_grad = (hidden_grad * activated).astype(jnp.bfloat16)
    gate_grad = (hidden_grad * up_val * sigmoid_gate * (1.0 + gate * (1.0 - sigmoid_gate))).astype(
        jnp.bfloat16
    )
    return hidden, gate_grad, up_grad


def units_kernel(in_ref, grad_ref, gate_sum, up_sum, down_sum, gate_ref, up_ref, terms_ref, rows_ref, total_ref):
    step = pl.program_id(0)
    hidden, gate_grad, up_grad = backward_units(
        *(part[...].astype(jnp.float32) for part in (gate_sum, up_sum, down_sum))
    )
    for k, (rows, units) in enumerate(((in_ref, gate_grad), (in_ref, up_grad), (grad_ref, hidden))):
        terms_ref[k] = jnp.dot(rows[...], units, preferred_element_type=jnp.float32).astype(jnp.bfloat16)
    part = lax.dot_general(
        gate_grad, gate_ref[...], CONTRACT_UNITS, preferred_element_type=jnp.float32
    ) + lax.dot_general(up_grad, up_ref[...], CONTRACT_UNITS, preferred_element_type=jnp.float32)

    @pl.when(step == 0)
    def _():
        total_ref[...] = part

    @pl.when(step > 0)
    def _():
        total_ref[...] += part

    @pl.when(step == pl.num_programs(0) - 1)
    def _():
        rows_ref[...] = total_ref[...].astype(jnp.bfloat16)


def unit_terms(in_t, grad_t, sums, gate_w, up_w):
    width, rows = in_t.shape
    count = gate_w.shape[1]
    whole = pl.BlockSpec((width, rows), lambda i: (0, 0))
    part = pl.BlockSpec((rows, BLOCK), lambda i: (0, i))
    weight = pl.BlockSpec((width, BLOCK), lambda i: (0, i))
    return pl.pallas_call(
        units_kernel,
        grid=(count // BLOCK,),
        in_specs=[whole, whole, part, part, part, weight, weight],
        out_specs=[
            pl.BlockSpec((3, width, BLOCK), lambda i: (0, 0, i)),
            pl.BlockSpec((rows, width), lambda i: (0, 0)),
        ],
        out_shape=[
            jax.ShapeDtypeStruct((3, width, count), jnp.bfloat16),
            jax.ShapeDtypeStruct((rows, width), jnp.bfloat16),
        ],
        scratch_shapes=[pltpu.VMEM((rows, width), jnp.float32)],
        compiler_params=pltpu.CompilerParams(vmem_limit_bytes=60 * 2**20),
        cost_estimate=pl.CostEstimate(
            flops=10 * rows * width * count, bytes_accessed=20 * 2**20, transcendentals=rows * count
        ),
        name="unit_terms",
    )(in_t, grad_t, *sums, gate_w, up_w)


def which_pairing(plan, tables):
    replicas = plan.shape[0]
    same = (plan[:, None] == plan[None, :]) & ~np.eye(replicas, dtype=bool)
    ids = jnp.arange(replicas, dtype=jnp.int32)
    partner = ids + jnp.sum(jnp.where(same, ids[None, :] - ids[:, None], 0), axis=1)
    agree = jnp.all(jnp.asarray(tables, jnp.int32) == partner[None, :], axis=1)
    return jnp.sum(jnp.where(agree, jnp.arange(len(tables), dtype=jnp.int32), 0))


def swapped(partner, terms):
    count = len(partner)
    chips = count // CORES

    def apart(a, b):
        steps = (b // CORES - a // CORES) % chips
        return min(steps, chips - steps)

    def moved(value, pairs):
        return lax.ppermute(value, "ep", pairs)

    pairs = [(r, p) for r, p in enumerate(partner) if p != r]
    far = [(r, p) for r, p in pairs if apart(r, p) > 1]
    near = [(r, p) for r, p in pairs if apart(r, p) <= 1]
    if len(far) != 2 or all(apart(r, p) == 0 for r, p in near):
        return moved(terms, pairs)
    way = -CORES if far[0][0] // CORES % 2 == 0 else CORES
    first = [(r, (r + way) % count) for r, _ in far]
    second = [((r + way) % count, p) for r, p in far]
    flat = terms.reshape(-1, terms.shape[2])
    cut = flat.shape[0] // 7 * 3
    upper, lower = flat[:cut], flat[cut:]
    relayed = moved(moved(lower, first), second) + moved(lower, near)
    return jnp.concatenate([moved(upper, pairs), relayed], axis=0).reshape(terms.shape)


def from_partner(terms, index, tables):
    return lax.switch(index, [functools.partial(swapped, t) for t in tables], terms)


def on_device(tokens, grad_out, route_ids, route_probs, replica_pick, plan, w_gate, w_up, w_down):
    replicas = plan.shape[0]
    dp_count = lax.axis_size("dp")
    width = tokens.shape[1] // dp_count
    tables = pairings(replicas)
    index = which_pairing(plan, tables)
    send, sel = dispatch(tokens, grad_out, route_ids, route_probs, replica_pick, plan, dp_count)
    recv = lax.all_to_all(
        send.reshape(replicas * dp_count, PAD, 2 * width),
        ("ep", "dp"),
        split_axis=0,
        concat_axis=0,
        tiled=True,
    )
    rows = recv[:, :MOST].reshape(-1, 2 * width)
    rows_in, rows_grad = rows[:, :width], rows[:, width:]
    gate_w, up_w, down_w = w_gate[0], w_up[0], w_down[0]
    sums = lax.psum(
        tuple(
            p.astype(jnp.bfloat16)
            for p in (
                jnp.dot(rows_in, gate_w, preferred_element_type=jnp.float32),
                jnp.dot(rows_in, up_w, preferred_element_type=jnp.float32),
                lax.dot_general(rows_grad, down_w, CONTRACT_UNITS, preferred_element_type=jnp.float32),
            )
        ),
        "dp",
    )
    in_t, grad_t, index, sums = lax.optimization_barrier((rows_in.T, rows_grad.T, index, sums))
    terms, row_grads = unit_terms(in_t, grad_t, sums, gate_w, up_w)
    other = from_partner(terms, index, tables)
    grads = [added(terms[k], other[k]).astype(jnp.bfloat16) for k in range(3)]
    back = row_grads.reshape(replicas * dp_count, MOST, width)
    back = jnp.pad(back, ((0, 0), (0, PAD - MOST), (0, 0)))
    back = lax.all_to_all(back, ("ep", "dp"), split_axis=0, concat_axis=0, tiled=True)
    grad_tokens = combine(sel, back.reshape(replicas, dp_count, PAD, width))
    return grad_tokens, grads[0][None], grads[1][None], grads[2].T[None]


def solution(mesh):
    return jax.shard_map(
        on_device,
        mesh=mesh,
        in_specs=(
            P(("ep", "dp"), None),
            P(("ep", "dp"), None),
            P(("ep", "dp"), None),
            P(("ep", "dp"), None),
            P(("ep", "dp"), None),
            P(),
            P("ep", "dp", None),
            P("ep", "dp", None),
            P("ep", None, "dp"),
        ),
        out_specs=(
            P(("ep", "dp"), None),
            P("ep", "dp", None),
            P("ep", "dp", None),
            P("ep", None, "dp"),
        ),
        check_vma=False,
    )
```

```python
import functools
import itertools

import jax
import jax.numpy as jnp
import numpy as np
from jax import lax
from jax.experimental import pallas as pl
from jax.experimental.pallas import tpu as pltpu
from jax.sharding import PartitionSpec as P

MOST = 6
PAD = 8
BLOCK = 256
CORES = 2
CONTRACT_ROWS = (((0,), (0,)), ((), ()))
CONTRACT_UNITS = (((1,), (1,)), ((), ()))


def pairings(replicas):
    tables = []
    pairs = list(itertools.combinations(range(replicas), 2))
    for first, second in itertools.combinations(pairs, 2):
        if not set(first) & set(second):
            partner = list(range(replicas))
            for a, b in (first, second):
                partner[a], partner[b] = b, a
            tables.append(partner)
    return tables


def dispatch_kernel(ids_ref, pick_ref, probs_ref, plan_ref, tok_ref, grad_ref, send_ref, sel_ref, scale_ref):
    replicas = plan_ref.shape[0]
    tokens = ids_ref.shape[1]

    @pl.when(pl.program_id(0) == 0)
    def _():
        ids = ids_ref[...]
        pick = pick_ref[...]
        probs = probs_ref[...]
        hits, weights = [], []
        for r in range(replicas):
            expert = plan_ref[r]
            copies = jnp.int32(0)
            rank = jnp.int32(0)
            for other in range(replicas):
                same = (plan_ref[other] == expert).astype(jnp.int32)
                copies += same
                if other < r:
                    rank += same
            wanted = jnp.where(copies > 1, lax.rem(pick, jnp.int32(2)), 0)
            matched = (ids == expert) & (wanted == rank)
            hits.append(jnp.max(jnp.where(matched, 1.0, 0.0), axis=0, keepdims=True))
            weights.append(jnp.sum(jnp.where(matched, probs, 0.0), axis=0, keepdims=True))
        hit = jnp.concatenate(hits, axis=0)
        earlier = lax.broadcasted_iota(jnp.int32, (tokens, tokens), 0) < lax.broadcasted_iota(
            jnp.int32, (tokens, tokens), 1
        )
        before = jnp.dot(
            hit.astype(jnp.bfloat16),
            earlier.astype(jnp.float32).astype(jnp.bfloat16),
            preferred_element_type=jnp.float32,
        )
        slot = lax.broadcasted_iota(jnp.int32, (PAD, tokens), 0).astype(jnp.float32)
        rows, scales = [], []
        for r in range(replicas):
            chosen = jnp.where((before[r : r + 1] == slot) & (hit[r : r + 1] > 0.0), 1.0, 0.0)
            rows.append(chosen)
            scales.append(jnp.sum(chosen * weights[r], axis=1, keepdims=True))
        sel_ref[...] = jnp.concatenate(rows, axis=0).astype(jnp.bfloat16)
        scale_ref[...] = jnp.broadcast_to(jnp.concatenate(scales, axis=0), scale_ref.shape)

    sel = sel_ref[...]
    rows_in = jnp.dot(sel, tok_ref[...], preferred_element_type=jnp.float32)
    rows_grad = jnp.dot(sel, grad_ref[...], preferred_element_type=jnp.float32) * scale_ref[:, :1]
    width = send_ref.shape[3] // 2
    for b in range(send_ref.shape[1]):
        cols = slice(b * width, (b + 1) * width)
        both = jnp.concatenate([rows_in[:, cols], rows_grad[:, cols]], axis=1)
        send_ref[:, b] = both.reshape(replicas, PAD, 2 * width).astype(jnp.bfloat16)


def dispatch(tokens, grad_out, route_ids, route_probs, replica_pick, plan, dp_count):
    count, model_width = tokens.shape
    replicas = plan.shape[0]
    width = model_width // dp_count
    top = route_ids.shape[1]
    step = dp_count // 4
    small = pl.BlockSpec((top, count), lambda i: (0, 0))
    return pl.pallas_call(
        dispatch_kernel,
        grid=(dp_count // step,),
        in_specs=[
            small,
            small,
            small,
            pl.BlockSpec(memory_space=pltpu.SMEM),
            pl.BlockSpec((count, step * width), lambda i: (0, i)),
            pl.BlockSpec((count, step * width), lambda i: (0, i)),
        ],
        out_specs=[
            pl.BlockSpec((replicas, step, PAD, 2 * width), lambda i: (0, i, 0, 0)),
            pl.BlockSpec((replicas * PAD, count), lambda i: (0, 0)),
        ],
        out_shape=[
            jax.ShapeDtypeStruct((replicas, dp_count, PAD, 2 * width), jnp.bfloat16),
            jax.ShapeDtypeStruct((replicas * PAD, count), jnp.bfloat16),
        ],
        scratch_shapes=[pltpu.VMEM((replicas * PAD, 128), jnp.float32)],
        compiler_params=pltpu.CompilerParams(vmem_limit_bytes=60 * 2**20),
        name="dispatch",
    )(route_ids.T, replica_pick.T, route_probs.T, plan, tokens, grad_out)


def combine_kernel(sel_ref, back_ref, out_ref):
    sel = sel_ref[...]
    parts = []
    for b in range(back_ref.shape[1]):
        rows = back_ref[:, b].astype(jnp.float32).reshape(-1, back_ref.shape[3]).astype(jnp.bfloat16)
        parts.append(lax.dot_general(sel, rows, CONTRACT_ROWS, preferred_element_type=jnp.float32))
    out_ref[...] = jnp.concatenate(parts, axis=1).astype(jnp.bfloat16)


def combine(sel, back):
    slots, count = sel.shape
    replicas, dp_count, pad, width = back.shape
    step = dp_count // 2
    return pl.pallas_call(
        combine_kernel,
        grid=(dp_count // step,),
        in_specs=[
            pl.BlockSpec((slots, count), lambda i: (0, 0)),
            pl.BlockSpec((replicas, step, pad, width), lambda i: (0, i, 0, 0)),
        ],
        out_specs=pl.BlockSpec((count, step * width), lambda i: (0, i)),
        out_shape=jax.ShapeDtypeStruct((count, dp_count * width), jnp.bfloat16),
        compiler_params=pltpu.CompilerParams(vmem_limit_bytes=32 * 2**20),
        name="combine",
    )(sel, back)


def added(first, *others):
    total = first.astype(jnp.float32)
    for other in others:
        total = total + other.astype(jnp.float32)
    return total


def backward_units(gate, up_val, hidden_grad):
    sigmoid_gate = jax.nn.sigmoid(gate)
    activated = gate * sigmoid_gate
    hidden = (activated * up_val).astype(jnp.bfloat16)
    up_grad = (hidden_grad * activated).astype(jnp.bfloat16)
    gate_grad = (hidden_grad * up_val * sigmoid_gate * (1.0 + gate * (1.0 - sigmoid_gate))).astype(
        jnp.bfloat16
    )
    return hidden, gate_grad, up_grad


def units_kernel(in_ref, grad_ref, gate_sum, up_sum, down_sum, gate_ref, up_ref, terms_ref, rows_ref, total_ref):
    step = pl.program_id(0)
    hidden, gate_grad, up_grad = backward_units(
        *(part[...].astype(jnp.float32) for part in (gate_sum, up_sum, down_sum))
    )
    for k, (rows, units) in enumerate(((in_ref, gate_grad), (in_ref, up_grad), (grad_ref, hidden))):
        terms_ref[k] = jnp.dot(rows[...], units, preferred_element_type=jnp.float32).astype(jnp.bfloat16)
    part = lax.dot_general(
        gate_grad, gate_ref[...], CONTRACT_UNITS, preferred_element_type=jnp.float32
    ) + lax.dot_general(up_grad, up_ref[...], CONTRACT_UNITS, preferred_element_type=jnp.float32)

    @pl.when(step == 0)
    def _():
        total_ref[...] = part

    @pl.when(step > 0)
    def _():
        total_ref[...] += part

    @pl.when(step == pl.num_programs(0) - 1)
    def _():
        rows_ref[...] = total_ref[...].astype(jnp.bfloat16)


def unit_terms(in_t, grad_t, sums, gate_w, up_w):
    width, rows = in_t.shape
    count = gate_w.shape[1]
    whole = pl.BlockSpec((width, rows), lambda i: (0, 0))
    part = pl.BlockSpec((rows, BLOCK), lambda i: (0, i))
    weight = pl.BlockSpec((width, BLOCK), lambda i: (0, i))
    return pl.pallas_call(
        units_kernel,
        grid=(count // BLOCK,),
        in_specs=[whole, whole, part, part, part, weight, weight],
        out_specs=[
            pl.BlockSpec((3, width, BLOCK), lambda i: (0, 0, i)),
            pl.BlockSpec((rows, width), lambda i: (0, 0)),
        ],
        out_shape=[
            jax.ShapeDtypeStruct((3, width, count), jnp.bfloat16),
            jax.ShapeDtypeStruct((rows, width), jnp.bfloat16),
        ],
        scratch_shapes=[pltpu.VMEM((rows, width), jnp.float32)],
        compiler_params=pltpu.CompilerParams(vmem_limit_bytes=60 * 2**20),
        cost_estimate=pl.CostEstimate(
            flops=10 * rows * width * count, bytes_accessed=20 * 2**20, transcendentals=rows * count
        ),
        name="unit_terms",
    )(in_t, grad_t, *sums, gate_w, up_w)


def which_pairing(plan, tables):
    replicas = plan.shape[0]
    same = (plan[:, None] == plan[None, :]) & ~np.eye(replicas, dtype=bool)
    ids = jnp.arange(replicas, dtype=jnp.int32)
    partner = ids + jnp.sum(jnp.where(same, ids[None, :] - ids[:, None], 0), axis=1)
    agree = jnp.all(jnp.asarray(tables, jnp.int32) == partner[None, :], axis=1)
    return jnp.sum(jnp.where(agree, jnp.arange(len(tables), dtype=jnp.int32), 0))


def swapped(partner, terms):
    count = len(partner)
    chips = count // CORES

    def apart(a, b):
        steps = (b // CORES - a // CORES) % chips
        return min(steps, chips - steps)

    def moved(value, pairs):
        return lax.ppermute(value, "ep", pairs)

    pairs = [(r, p) for r, p in enumerate(partner) if p != r]
    far = [(r, p) for r, p in pairs if apart(r, p) > 1]
    near = [(r, p) for r, p in pairs if apart(r, p) <= 1]
    if len(far) != 2 or all(apart(r, p) == 0 for r, p in near):
        return moved(terms, pairs)
    way = -1 if far[0][0] // CORES % 2 == 0 else 1
    busy = [r for r, _ in near]
    first, second = [], []
    for r, p in far:
        chip = (r // CORES + way) % chips
        between = next(d for d in range(chip * CORES, (chip + 1) * CORES) if d not in busy)
        first.append((r, between))
        second.append((between, p))
    flat = terms.reshape(-1, terms.shape[2])
    cut = flat.shape[0] // 7 * 3
    here = lax.axis_index("ep")
    once = moved(flat[cut:], first + near)
    twice = moved(once, second)
    am_near = functools.reduce(jnp.logical_or, [here == r for r in busy])
    lower = jnp.where(am_near, once, twice)
    return jnp.concatenate([moved(flat[:cut], pairs), lower], axis=0).reshape(terms.shape)


def from_partner(terms, index, tables):
    return lax.switch(index, [functools.partial(swapped, t) for t in tables], terms)


def on_device(tokens, grad_out, route_ids, route_probs, replica_pick, plan, w_gate, w_up, w_down):
    replicas = plan.shape[0]
    dp_count = lax.axis_size("dp")
    width = tokens.shape[1] // dp_count
    tables = pairings(replicas)
    index = which_pairing(plan, tables)
    send, sel = dispatch(tokens, grad_out, route_ids, route_probs, replica_pick, plan, dp_count)
    recv = lax.all_to_all(
        send.reshape(replicas * dp_count, PAD, 2 * width),
        ("ep", "dp"),
        split_axis=0,
        concat_axis=0,
        tiled=True,
    )
    rows = recv[:, :MOST].reshape(-1, 2 * width)
    rows_in, rows_grad = rows[:, :width], rows[:, width:]
    gate_w, up_w, down_w = w_gate[0], w_up[0], w_down[0]
    sums = lax.psum(
        tuple(
            p.astype(jnp.bfloat16)
            for p in (
                jnp.dot(rows_in, gate_w, preferred_element_type=jnp.float32),
                jnp.dot(rows_in, up_w, preferred_element_type=jnp.float32),
                lax.dot_general(rows_grad, down_w, CONTRACT_UNITS, preferred_element_type=jnp.float32),
            )
        ),
        "dp",
    )
    in_t, grad_t, index, sums = lax.optimization_barrier((rows_in.T, rows_grad.T, index, sums))
    terms, row_grads = unit_terms(in_t, grad_t, sums, gate_w, up_w)
    other = from_partner(terms, index, tables)
    grads = [added(terms[k], other[k]).astype(jnp.bfloat16) for k in range(3)]
    back = row_grads.reshape(replicas * dp_count, MOST, width)
    back = jnp.pad(back, ((0, 0), (0, PAD - MOST), (0, 0)))
    back = lax.all_to_all(back, ("ep", "dp"), split_axis=0, concat_axis=0, tiled=True)
    grad_tokens = combine(sel, back.reshape(replicas, dp_count, PAD, width))
    return grad_tokens, grads[0][None], grads[1][None], grads[2].T[None]


def solution(mesh):
    return jax.shard_map(
        on_device,
        mesh=mesh,
        in_specs=(
            P(("ep", "dp"), None),
            P(("ep", "dp"), None),
            P(("ep", "dp"), None),
            P(("ep", "dp"), None),
            P(("ep", "dp"), None),
            P(),
            P("ep", "dp", None),
            P("ep", "dp", None),
            P("ep", None, "dp"),
        ),
        out_specs=(
            P(("ep", "dp"), None),
            P("ep", "dp", None),
            P("ep", "dp", None),
            P("ep", None, "dp"),
        ),
        check_vma=False,
    )
```

```python
import functools
import itertools

import jax
import jax.numpy as jnp
import numpy as np
from jax import lax
from jax.experimental import pallas as pl
from jax.experimental.pallas import tpu as pltpu
from jax.sharding import PartitionSpec as P

MOST = 6
PAD = 8
BLOCK = 256
CONTRACT_ROWS = (((0,), (0,)), ((), ()))
CONTRACT_UNITS = (((1,), (1,)), ((), ()))


def pairings(replicas):
    tables = []
    pairs = list(itertools.combinations(range(replicas), 2))
    for first, second in itertools.combinations(pairs, 2):
        if not set(first) & set(second):
            partner = list(range(replicas))
            for a, b in (first, second):
                partner[a], partner[b] = b, a
            tables.append(partner)
    return tables


def dispatch_kernel(ids_ref, pick_ref, probs_ref, plan_ref, tok_ref, grad_ref, send_ref, sel_ref, scale_ref):
    replicas = plan_ref.shape[0]
    tokens = ids_ref.shape[1]

    @pl.when(pl.program_id(0) == 0)
    def _():
        ids = ids_ref[...]
        pick = pick_ref[...]
        probs = probs_ref[...]
        hits, weights = [], []
        for r in range(replicas):
            expert = plan_ref[r]
            copies = jnp.int32(0)
            rank = jnp.int32(0)
            for other in range(replicas):
                same = (plan_ref[other] == expert).astype(jnp.int32)
                copies += same
                if other < r:
                    rank += same
            wanted = jnp.where(copies > 1, lax.rem(pick, jnp.int32(2)), 0)
            matched = (ids == expert) & (wanted == rank)
            hits.append(jnp.max(jnp.where(matched, 1.0, 0.0), axis=0, keepdims=True))
            weights.append(jnp.sum(jnp.where(matched, probs, 0.0), axis=0, keepdims=True))
        hit = jnp.concatenate(hits, axis=0)
        earlier = lax.broadcasted_iota(jnp.int32, (tokens, tokens), 0) < lax.broadcasted_iota(
            jnp.int32, (tokens, tokens), 1
        )
        before = jnp.dot(
            hit.astype(jnp.bfloat16),
            earlier.astype(jnp.float32).astype(jnp.bfloat16),
            preferred_element_type=jnp.float32,
        )
        slot = lax.broadcasted_iota(jnp.int32, (PAD, tokens), 0).astype(jnp.float32)
        rows, scales = [], []
        for r in range(replicas):
            chosen = jnp.where((before[r : r + 1] == slot) & (hit[r : r + 1] > 0.0), 1.0, 0.0)
            rows.append(chosen)
            scales.append(jnp.sum(chosen * weights[r], axis=1, keepdims=True))
        sel_ref[...] = jnp.concatenate(rows, axis=0).astype(jnp.bfloat16)
        scale_ref[...] = jnp.broadcast_to(jnp.concatenate(scales, axis=0), scale_ref.shape)

    sel = sel_ref[...]
    rows_in = jnp.dot(sel, tok_ref[...], preferred_element_type=jnp.float32)
    rows_grad = jnp.dot(sel, grad_ref[...], preferred_element_type=jnp.float32) * scale_ref[:, :1]
    width = send_ref.shape[3] // 2
    for b in range(send_ref.shape[1]):
        cols = slice(b * width, (b + 1) * width)
        both = jnp.concatenate([rows_in[:, cols], rows_grad[:, cols]], axis=1)
        send_ref[:, b] = both.reshape(replicas, PAD, 2 * width).astype(jnp.bfloat16)


def dispatch(tokens, grad_out, route_ids, route_probs, replica_pick, plan, dp_count):
    count, model_width = tokens.shape
    replicas = plan.shape[0]
    width = model_width // dp_count
    top = route_ids.shape[1]
    step = dp_count // 4
    small = pl.BlockSpec((top, count), lambda i: (0, 0))
    return pl.pallas_call(
        dispatch_kernel,
        grid=(dp_count // step,),
        in_specs=[
            small,
            small,
            small,
            pl.BlockSpec(memory_space=pltpu.SMEM),
            pl.BlockSpec((count, step * width), lambda i: (0, i)),
            pl.BlockSpec((count, step * width), lambda i: (0, i)),
        ],
        out_specs=[
            pl.BlockSpec((replicas, step, PAD, 2 * width), lambda i: (0, i, 0, 0)),
            pl.BlockSpec((replicas * PAD, count), lambda i: (0, 0)),
        ],
        out_shape=[
            jax.ShapeDtypeStruct((replicas, dp_count, PAD, 2 * width), jnp.bfloat16),
            jax.ShapeDtypeStruct((replicas * PAD, count), jnp.bfloat16),
        ],
        scratch_shapes=[pltpu.VMEM((replicas * PAD, 128), jnp.float32)],
        compiler_params=pltpu.CompilerParams(vmem_limit_bytes=60 * 2**20),
        name="dispatch",
    )(route_ids.T, replica_pick.T, route_probs.T, plan, tokens, grad_out)


def combine_kernel(sel_ref, back_ref, out_ref):
    sel = sel_ref[...]
    parts = []
    for b in range(back_ref.shape[1]):
        rows = back_ref[:, b].astype(jnp.float32).reshape(-1, back_ref.shape[3]).astype(jnp.bfloat16)
        parts.append(lax.dot_general(sel, rows, CONTRACT_ROWS, preferred_element_type=jnp.float32))
    out_ref[...] = jnp.concatenate(parts, axis=1).astype(jnp.bfloat16)


def combine(sel, back):
    slots, count = sel.shape
    replicas, dp_count, pad, width = back.shape
    step = dp_count // 2
    return pl.pallas_call(
        combine_kernel,
        grid=(dp_count // step,),
        in_specs=[
            pl.BlockSpec((slots, count), lambda i: (0, 0)),
            pl.BlockSpec((replicas, step, pad, width), lambda i: (0, i, 0, 0)),
        ],
        out_specs=pl.BlockSpec((count, step * width), lambda i: (0, i)),
        out_shape=jax.ShapeDtypeStruct((count, dp_count * width), jnp.bfloat16),
        compiler_params=pltpu.CompilerParams(vmem_limit_bytes=32 * 2**20),
        name="combine",
    )(sel, back)


def added(first, *others):
    total = first.astype(jnp.float32)
    for other in others:
        total = total + other.astype(jnp.float32)
    return total


def backward_units(gate, up_val, hidden_grad):
    sigmoid_gate = jax.nn.sigmoid(gate)
    activated = gate * sigmoid_gate
    hidden = (activated * up_val).astype(jnp.bfloat16)
    up_grad = (hidden_grad * activated).astype(jnp.bfloat16)
    gate_grad = (hidden_grad * up_val * sigmoid_gate * (1.0 + gate * (1.0 - sigmoid_gate))).astype(
        jnp.bfloat16
    )
    return hidden, gate_grad, up_grad


def units_kernel(in_ref, grad_ref, gate_sum, up_sum, down_sum, gate_ref, up_ref, terms_ref, rows_ref, total_ref):
    step = pl.program_id(0)
    hidden, gate_grad, up_grad = backward_units(
        *(part[...].astype(jnp.float32) for part in (gate_sum, up_sum, down_sum))
    )
    for k, (rows, units) in enumerate(((in_ref, gate_grad), (in_ref, up_grad), (grad_ref, hidden))):
        terms_ref[k] = jnp.dot(rows[...], units, preferred_element_type=jnp.float32).astype(jnp.bfloat16)
    part = lax.dot_general(
        gate_grad, gate_ref[...], CONTRACT_UNITS, preferred_element_type=jnp.float32
    ) + lax.dot_general(up_grad, up_ref[...], CONTRACT_UNITS, preferred_element_type=jnp.float32)

    @pl.when(step == 0)
    def _():
        total_ref[...] = part

    @pl.when(step > 0)
    def _():
        total_ref[...] += part

    @pl.when(step == pl.num_programs(0) - 1)
    def _():
        rows_ref[...] = total_ref[...].astype(jnp.bfloat16)


def unit_terms(in_t, grad_t, sums, gate_w, up_w):
    width, rows = in_t.shape
    count = gate_w.shape[1]
    whole = pl.BlockSpec((width, rows), lambda i: (0, 0))
    part = pl.BlockSpec((rows, BLOCK), lambda i: (0, i))
    weight = pl.BlockSpec((width, BLOCK), lambda i: (0, i))
    return pl.pallas_call(
        units_kernel,
        grid=(count // BLOCK,),
        in_specs=[whole, whole, part, part, part, weight, weight],
        out_specs=[
            pl.BlockSpec((3, width, BLOCK), lambda i: (0, 0, i)),
            pl.BlockSpec((rows, width), lambda i: (0, 0)),
        ],
        out_shape=[
            jax.ShapeDtypeStruct((3, width, count), jnp.bfloat16),
            jax.ShapeDtypeStruct((rows, width), jnp.bfloat16),
        ],
        scratch_shapes=[pltpu.VMEM((rows, width), jnp.float32)],
        compiler_params=pltpu.CompilerParams(vmem_limit_bytes=60 * 2**20),
        cost_estimate=pl.CostEstimate(
            flops=10 * rows * width * count, bytes_accessed=20 * 2**20, transcendentals=rows * count
        ),
        name="unit_terms",
    )(in_t, grad_t, *sums, gate_w, up_w)


def which_pairing(plan, tables):
    replicas = plan.shape[0]
    same = (plan[:, None] == plan[None, :]) & ~np.eye(replicas, dtype=bool)
    ids = jnp.arange(replicas, dtype=jnp.int32)
    partner = ids + jnp.sum(jnp.where(same, ids[None, :] - ids[:, None], 0), axis=1)
    agree = jnp.all(jnp.asarray(tables, jnp.int32) == partner[None, :], axis=1)
    return jnp.sum(jnp.where(agree, jnp.arange(len(tables), dtype=jnp.int32), 0))


def from_partner(terms, index, tables):
    def branch(partner, value):
        return lax.ppermute(value, "ep", [(r, p) for r, p in enumerate(partner) if p != r])

    return lax.switch(index, [functools.partial(branch, t) for t in tables], terms)


def on_device(tokens, grad_out, route_ids, route_probs, replica_pick, plan, w_gate, w_up, w_down):
    replicas = plan.shape[0]
    dp_count = lax.axis_size("dp")
    width = tokens.shape[1] // dp_count
    tables = pairings(replicas)
    index = which_pairing(plan, tables)
    send, sel = dispatch(tokens, grad_out, route_ids, route_probs, replica_pick, plan, dp_count)
    recv = lax.all_to_all(
        send.reshape(replicas * dp_count, PAD, 2 * width),
        ("ep", "dp"),
        split_axis=0,
        concat_axis=0,
        tiled=True,
    )
    rows = recv[:, :MOST].reshape(-1, 2 * width)
    rows_in, rows_grad = rows[:, :width], rows[:, width:]
    gate_w, up_w, down_w = w_gate[0], w_up[0], w_down[0]
    sums = lax.psum(
        tuple(
            p.astype(jnp.bfloat16)
            for p in (
                jnp.dot(rows_in, gate_w, preferred_element_type=jnp.float32),
                jnp.dot(rows_in, up_w, preferred_element_type=jnp.float32),
                lax.dot_general(rows_grad, down_w, CONTRACT_UNITS, preferred_element_type=jnp.float32),
            )
        ),
        "dp",
    )
    in_t, grad_t, index, sums = lax.optimization_barrier((rows_in.T, rows_grad.T, index, sums))
    terms, row_grads = unit_terms(in_t, grad_t, sums, gate_w, up_w)
    other = from_partner(terms, index, tables)
    grads = [added(terms[k], other[k]).astype(jnp.bfloat16) for k in range(3)]
    back = row_grads.reshape(replicas * dp_count, MOST, width)
    back = jnp.pad(back, ((0, 0), (0, PAD - MOST), (0, 0)))
    back = lax.all_to_all(back, ("ep", "dp"), split_axis=0, concat_axis=0, tiled=True)
    grad_tokens = combine(sel, back.reshape(replicas, dp_count, PAD, width))
    return grad_tokens, grads[0][None], grads[1][None], grads[2].T[None]


def solution(mesh):
    return jax.shard_map(
        on_device,
        mesh=mesh,
        in_specs=(
            P(("ep", "dp"), None),
            P(("ep", "dp"), None),
            P(("ep", "dp"), None),
            P(("ep", "dp"), None),
            P(("ep", "dp"), None),
            P(),
            P("ep", "dp", None),
            P("ep", "dp", None),
            P("ep", None, "dp"),
        ),
        out_specs=(
            P(("ep", "dp"), None),
            P("ep", "dp", None),
            P("ep", "dp", None),
            P("ep", None, "dp"),
        ),
        check_vma=False,
    )
```
